512 devices in a mesh: section: 8 (over z_hi, core), expert: 64 (over x, y, z_lo).
Axes of the slice: x: 4, y: 4, z: 16 (z_hi: 4, z_lo: 4; z = z_hi * 4 + z_lo), core: 2. Of those that a mesh axis runs over, the one named last changes fastest.
Arguments:
- hidden_rows: bfloat16 [8, 4096, 3584], P('section', 'expert'), may hold values from -6 to 6
- norm_gain: float32 [8, 3584], P('section'), may hold values from 0.1 to 1.9
- routes: int32 [8, 4096, 2], P('section', 'expert'), may hold values from 0 to 7, all different within a row; in each aligned block of 64 rows (0 to 63, 64 to 127, ..., all dimensions but the last counted through in order) at most 16 rows name the same one
- gates: float32 [8, 4096, 2], P('section', 'expert'), may hold values from 0.1 to 0.6
- w_gate_up: bfloat16 [8, 64, 3584, 256], P('section', 'expert'), may hold values from -0.09375 to 0.09375
- w_down: bfloat16 [8, 64, 128, 3584], P('section', 'expert'), may hold values from -0.1875 to 0.1875
Outputs:
- handoff: bfloat16 [8, 4096, 3584], P('section', 'expert')
The draws below stay inside these ranges and needn't reach their ends.
Inputs may be any that keep to these rules, and one draw needn't show every extreme that they name: `routes`: in the rows of one device, every expert is named exactly 16 times.
All inputs are finite; a program needn't handle non-finite values.
Results may differ from the reference program's by a relative error of at most 0.004.
Values may be sent and summed in bfloat16 or wider, within the bound.
A program may use at most 64 MiB of HBM per device.

```python
import math
import jax
import jax.numpy as jnp
import numpy as np
from jax import lax

D = 3584
EF_DEV = 128
EXPERTS = 8
TOP = 2
TOK_DEV = 64
SHARDS = 8
EF = 1024
TOKENS = 4096
CAP = 16
N_SECTION = 8
N_EXPERT = 64


def block_scale(own_key, dims, cuts, smallest, largest):
    def one(position, shards_of):
        heights = jax.random.uniform(jax.random.fold_in(jax.random.fold_in(own_key, 6), position), (shards_of,), jnp.float32, smallest / len(cuts), largest / len(cuts))
        return jnp.repeat(jnp.exp(heights), dims[position] // shards_of).reshape((-1,) + (1,) * (len(dims) - position - 1))

    factor_of = one(*cuts[0])
    for cut in cuts[1:]:
        factor_of = factor_of * one(*cut)
    return factor_of


def assign_block(key, own, number, rows, amount, top, limit, skew):
    ranking = jax.random.permutation(key, amount)
    packed, common = portions_of(amount, rows * top, limit, skew, True), portions_of(amount, rows * top, limit, skew, False)
    places = jnp.arange(amount)

    def named(tallies, offset_by):
        used = int((tallies > 0).sum())
        fixed = max(1, used // 4)
        moved = fixed + (places - fixed + offset_by * (used - fixed)) % max(1, amount - fixed)
        return jnp.zeros((amount,), jnp.int32).at[ranking[jnp.where(places < fixed, places, moved)]].set(jnp.asarray(tallies, jnp.int32))

    tallies = jnp.where(number % 4 == 0, named(packed, number // 4), named(common, number - number // 4 - 1))
    mixed = jax.random.permutation(jax.random.fold_in(own, 3), amount)
    donor, taker = mixed[0:amount // 2 * 2:2], mixed[1:amount // 2 * 2:2]
    slack = jnp.minimum(tallies[donor] - 1, limit - tallies[taker]) // 2
    slack = jnp.where((donor == ranking[0]) | (taker == ranking[0]) | (tallies[taker] == 0), 0, jnp.maximum(slack, 0))
    moved = jax.random.randint(jax.random.fold_in(own, 4), (amount // 2,), 0, 1 << 20) % (slack + 1)
    tallies = tallies.at[donor].add(-moved).at[taker].add(moved)
    labels = jnp.searchsorted(jnp.cumsum(tallies), jnp.arange(rows * top), side="right").astype(jnp.int32)
    grid = labels.reshape(top, rows).T
    grid = grid[jax.random.permutation(jax.random.fold_in(own, 1), rows)]
    offset_by = jax.random.randint(jax.random.fold_in(own, 2), (rows, 1), 0, top)
    return jnp.take_along_axis(grid, (jnp.arange(top)[None, :] + offset_by) % top, axis=1)


def portions_of(amount, total, most, lean, full):
    loads = [(1 << 20) // math.isqrt(grade ** lean) + 1 for grade in range(1, amount + 1)]
    largest = most if full else min(most, max(-(-total // amount), total * loads[0] // sum(loads)))
    least = 1 if total - largest >= amount - 1 else 0
    given, spare = [largest] + [least] * (amount - 1), total - largest - least * (amount - 1)
    while spare > 0:
        candidates = [i for i in range(1, amount) if given[i] < largest] or [i for i in range(1, amount) if given[i] < most]
        whole, budget = sum([loads[i] for i in candidates]), spare
        for i in candidates:
            extra = min(most - given[i], max(1, budget * loads[i] // whole), spare)
            given[i] = given[i] + extra
            spare = spare - extra
    return np.array(given)


def normal_values(rng, extent, width, reach, cuts=(), held_as=jnp.bfloat16):
    level = block_scale(rng, extent, cuts, -0.22, 0.18) if cuts else 1.0
    entries = jax.random.normal(rng, extent, jnp.float32) * width * level
    return jnp.minimum(jnp.maximum(entries, -reach), reach).astype(held_as)


def setup_inputs(seed: int = 0) -> dict:
    keys = jax.random.split(jax.random.key(seed), 7)
    hidden_rows = normal_values(keys[0], (N_SECTION, TOKENS, D), 1.0, 6.0, ((0, 8), (1, 64)))
    norm_gain = jnp.clip(1.0 + 0.18 * jax.random.normal(keys[1], (N_SECTION, D), jnp.float32), 0.1, 1.9)
    routes_keys = jax.random.split(jax.random.fold_in(keys[2], 1), N_SECTION * TOKENS // TOK_DEV)
    routes_turns = jax.random.permutation(jax.random.fold_in(keys[2], 3), N_SECTION * TOKENS // TOK_DEV)
    routes = jax.vmap(lambda own, number: assign_block(jax.random.fold_in(keys[2], 2), own, number, TOK_DEV, EXPERTS, TOP, CAP, 2))(routes_keys, routes_turns).reshape((N_SECTION, TOKENS, TOP))
    gates = jnp.clip(0.1 + 0.5 * jax.random.uniform(keys[3], (N_SECTION, TOKENS, TOP), jnp.float32) ** block_scale(keys[3], (N_SECTION, TOKENS, TOP), ((0, 8), (1, 64)), -0.2, 0.2), 0.1, 0.6)
    w_gate_up = normal_values(keys[4], (N_SECTION, N_EXPERT, D, 2 * EF_DEV), D ** -0.5, 0.09375, ((0, 8), (1, 64)))
    w_down = normal_values(keys[5], (N_SECTION, N_EXPERT, EF_DEV, D), EF ** -0.5, 0.1875, ((0, 8), (1, 64)))
    return {"hidden_rows": hidden_rows, "norm_gain": norm_gain, "routes": routes, "gates": gates, "w_gate_up": w_gate_up, "w_down": w_down}


def section_experts(rows_in, gain, chosen, weights, gate_up_all, down_all):
    rows_f32 = rows_in.astype(jnp.float32)
    normed = (rows_f32 * lax.rsqrt(lax.optimization_barrier(jnp.mean(rows_f32 * rows_f32, axis=1, keepdims=True)) + 1e-06) * gain[None, :]).astype(jnp.bfloat16)
    expert_ids = chosen.reshape(-1).astype(jnp.int32)
    pair_weight = weights.reshape(-1)
    holder = (jnp.arange(expert_ids.shape[0], dtype=jnp.int32) // TOP).astype(jnp.int32)

    def one_expert(summed, expert):
        order = jnp.argsort(jnp.where(expert_ids == expert, 0, 1).astype(jnp.int32), stable=True)[:CAP * N_EXPERT].astype(jnp.int32)
        usable = expert_ids[order] == expert
        token_ids = holder[order]
        picked = normed[token_ids]

        def one_shard(shard):
            index = (expert * SHARDS + shard).astype(jnp.int32)
            gate_up = jnp.dot(picked, gate_up_all[index], preferred_element_type=jnp.float32)
            activated = (jax.nn.silu(gate_up[:, :EF_DEV]) * gate_up[:, EF_DEV:]).astype(jnp.bfloat16)
            return jnp.dot(activated, down_all[index], preferred_element_type=jnp.float32).astype(jnp.bfloat16)
        pieces = lax.map(one_shard, jnp.arange(SHARDS, dtype=jnp.int32))
        expert_out = lax.optimization_barrier(jnp.sum(pieces.astype(jnp.float32), axis=0))
        factor = jnp.where(usable, pair_weight[order], 0.0)
        summed = summed.at[token_ids].add(factor[:, None] * expert_out)
        return (summed, None)
    start_sum = jnp.zeros((rows_in.shape[0], D), jnp.float32)
    routed_sum, unused = lax.scan(one_expert, start_sum, jnp.arange(EXPERTS, dtype=jnp.int32))
    return (rows_f32 + routed_sum).astype(jnp.bfloat16)

def reference(hidden_rows, norm_gain, routes, gates, w_gate_up, w_down):
    layer_out = lax.map(lambda group: section_experts(*group), (hidden_rows, norm_gain, routes, gates, w_gate_up, w_down))
    return jnp.roll(layer_out, 1, axis=0)
```

```python
import functools

import jax
import jax.numpy as jnp
from jax import lax
from jax.experimental import pallas as pl
from jax.experimental.pallas import tpu as pltpu
from jax.sharding import PartitionSpec as P

EXPERTS = 8
SHARDS = 8
PLANES = 4
SECTIONS = 8
COLUMN_PARTS = 2
TILE = 512
MESH = pl.DeviceIdType.MESH
BF16 = jnp.bfloat16
F32 = jnp.float32


def layer_kernel(
    hidden,
    gain,
    routes,
    gates,
    w_gate_up,
    w_down,
    out,
    raw,
    meta,
    sorted_rows,
    rows,
    gate_up_w,
    down_w,
    act,
    piece,
    back,
    part,
    home,
    layer_out,
    own_w_sem,
    w_send,
    w_recv,
    raw_send,
    raw_recv,
    meta_send,
    meta_recv,
    go_send,
    go_recv,
    back_send,
    back_recv,
    part_send,
    part_recv,
    hand_send,
    hand_recv,
):
    tokens, width = hidden.shape
    cap = rows.shape[2]
    inner = w_down.shape[0]
    slots = EXPERTS * cap
    span = width // COLUMN_PARTS

    section = lax.axis_index("section")
    me = lax.axis_index("expert")
    z = lax.rem(me, PLANES)
    column = lax.div(me, PLANES)
    y = lax.rem(column, 4)
    rank = lax.div(me, SHARDS)
    y_half, y_odd = lax.div(y, 2), lax.rem(y, 2)
    side = lax.rem(y_half + y_odd, 2)
    partner = (column - y_odd + 1 - y_odd) * PLANES + z
    after = lax.rem(section + 1, SECTIONS)
    before = lax.rem(section + SECTIONS - 1, SECTIONS)

    def in_plane(e):
        half = lax.rem(e, 2)
        return (lax.div(e, 2) * 4 + 2 * half + lax.rem(half + side, 2)) * PLANES + z

    def along_z(plane):
        return column * PLANES + plane

    def remote(src, dst, send, recv, to, to_section=None):
        return pltpu.make_async_remote_copy(
            src_ref=src,
            dst_ref=dst,
            send_sem=send,
            recv_sem=recv,
            device_id=(section if to_section is None else to_section, to),
            device_id_type=MESH,
        )

    own_gate_up = pltpu.make_async_copy(w_gate_up, gate_up_w.at[0], own_w_sem.at[0])
    own_down = pltpu.make_async_copy(w_down, down_w.at[pl.ds(0, inner)], own_w_sem.at[1])
    own_gate_up.start()
    own_down.start()

    barrier = pltpu.get_barrier_semaphore()

    def greet(to, to_section):
        pl.semaphore_signal(barrier, inc=1, device_id=(to_section, to), device_id_type=MESH)

    for i in range(1, PLANES):
        greet(along_z(lax.rem(z + i, PLANES)), section)
    for d in range(1, EXPERTS):
        greet(in_plane(lax.rem(rank + d, EXPERTS)), section)
    greet(partner, section)
    greet(me, after)
    greet(me, before)
    pl.semaphore_wait(barrier, PLANES - 1 + EXPERTS - 1 + 3)

    send_gate_up = remote(w_gate_up, gate_up_w.at[1], w_send.at[0], w_recv.at[0], partner)
    send_gate_up.start()
    send_down = remote(w_down, down_w.at[pl.ds(inner, inner)], w_send.at[1], w_recv.at[1], partner)
    send_down.start()

    rows_f32 = hidden[...].astype(F32)
    scale = lax.rsqrt(jnp.mean(rows_f32 * rows_f32, axis=1, keepdims=True) + 1e-06)
    raw[z] = (rows_f32 * scale * gain[...]).astype(BF16)

    lane = lax.broadcasted_iota(jnp.int32, (tokens, slots), 1)
    token = lax.broadcasted_iota(jnp.int32, (tokens, slots), 0)
    first, second = routes[:, 0:1], routes[:, 1:2]
    names_first, names_second = lane == first, lane == second
    one_hot = (jnp.where(names_first, 1.0, 0.0) + jnp.where(names_second, 1.0, 0.0)).astype(BF16)
    below = jnp.where(
        lax.broadcasted_iota(jnp.int32, (tokens, tokens), 0)
        > lax.broadcasted_iota(jnp.int32, (tokens, tokens), 1),
        1.0,
        0.0,
    ).astype(BF16)
    earlier = jnp.dot(below, one_hot, preferred_element_type=F32)
    place_first = first.astype(F32) * cap + jnp.sum(
        jnp.where(names_first, earlier, 0.0), axis=1, keepdims=True
    )
    place_second = second.astype(F32) * cap + jnp.sum(
        jnp.where(names_second, earlier, 0.0), axis=1, keepdims=True
    )
    lane_f32, token_f32 = lane.astype(F32), token.astype(F32)
    at_first, at_second = lane_f32 == place_first, lane_f32 == place_second
    slot_token = jnp.sum(
        jnp.where(at_first, token_f32, 0.0) + jnp.where(at_second, token_f32, 0.0),
        axis=0,
        keepdims=True,
    )
    slot_gate = jnp.sum(
        jnp.where(at_first, gates[:, 0:1], 0.0) + jnp.where(at_second, gates[:, 1:2], 0.0),
        axis=0,
        keepdims=True,
    )
    meta_row = lax.broadcasted_iota(jnp.int32, (8, slots), 0)
    meta[z] = jnp.where(meta_row == 0, slot_token, slot_gate)

    for i in range(1, PLANES):
        to = lax.rem(z + i, PLANES)
        remote(meta.at[z], meta.at[z], meta_send.at[to], meta_recv.at[z], along_z(to)).start()
        remote(raw.at[z], raw.at[z], raw_send.at[to], raw_recv.at[z], along_z(to)).start()

    def sort_and_send(i, plane):
        placed = jnp.where(token_f32 == meta[plane, 0:1, :], 1.0, 0.0).astype(BF16)
        for c in range(0, width, TILE):
            block = lax.dot_general(
                placed,
                raw[plane, :, c : c + TILE],
                (((0,), (0,)), ((), ())),
                preferred_element_type=F32,
            ).astype(BF16)
            sorted_rows[plane, :, :, c : c + TILE] = block.reshape(EXPERTS, cap, TILE)
        for d in range(1, EXPERTS):
            e = lax.rem(rank + d, EXPERTS)
            remote(
                sorted_rows.at[plane, e],
                rows.at[plane, rank],
                go_send.at[plane * EXPERTS + e],
                go_recv.at[plane * EXPERTS + rank],
                in_plane(e),
            ).start()
        rows[plane, rank] = sorted_rows[plane, rank]

    def dispatch(i, carry):
        plane = lax.rem(z + i, PLANES)
        from_z = along_z(plane)
        remote(meta.at[z], meta.at[plane], meta_send.at[plane], meta_recv.at[plane], from_z).wait_recv()
        remote(raw.at[z], raw.at[plane], raw_send.at[plane], raw_recv.at[plane], from_z).wait_recv()
        sort_and_send(i, plane)
        return carry

    sort_and_send(0, z)
    lax.fori_loop(1, PLANES, dispatch, 0)

    own_gate_up.wait()
    own_down.wait()

    def activated(plane, shard):
        gate_up = jnp.dot(
            rows[plane].reshape(slots, width), gate_up_w[shard], preferred_element_type=F32
        )
        gate, up = gate_up[:, :inner], gate_up[:, inner:]
        act[plane, :, shard * inner : (shard + 1) * inner] = (
            gate / (1.0 + jnp.exp(-gate)) * up
        ).astype(BF16)

    def own_shard(i, carry):
        plane = lax.rem(z + i, PLANES)
        for d in range(1, EXPERTS):
            e = lax.rem(rank + d, EXPERTS)
            remote(
                sorted_rows.at[plane, e],
                rows.at[plane, e],
                go_send.at[plane * EXPERTS + e],
                go_recv.at[plane * EXPERTS + e],
                in_plane(e),
            ).wait_recv()
        activated(plane, 0)
        return carry

    lax.fori_loop(0, PLANES, own_shard, 0)
    send_gate_up.wait_recv()

    def other_shard(i, carry):
        activated(lax.rem(z + i, PLANES), 1)
        return carry

    lax.fori_loop(0, PLANES, other_shard, 0)
    send_down.wait_recv()

    def cols(h):
        return pl.ds(h * span, span)

    def back_copy(plane, e, h, mine):
        return remote(
            piece.at[plane, e, :, cols(h)],
            back.at[plane, rank if mine else e, :, cols(h)],
            back_send.at[(h * PLANES + plane) * EXPERTS + e],
            back_recv.at[(h * PLANES + plane) * EXPERTS + (rank if mine else e)],
            in_plane(e),
        )

    for h in range(COLUMN_PARTS):

        def down(i, carry, h=h):
            plane = lax.rem(z + i, PLANES)
            block = jnp.dot(
                act[plane], down_w[:, h * span : (h + 1) * span], preferred_element_type=F32
            ).astype(BF16)
            piece[plane, :, :, h * span : (h + 1) * span] = block.reshape(EXPERTS, cap, span)
            for d in range(1, EXPERTS):
                back_copy(plane, lax.rem(rank + d, EXPERTS), h, True).start()
            back[plane, rank, :, h * span : (h + 1) * span] = piece[
                plane, rank, :, h * span : (h + 1) * span
            ]
            return carry

        lax.fori_loop(0, PLANES, down, 0)

    def part_copy(plane, h, mine):
        return remote(
            part.at[plane, :, cols(h)],
            home.at[z if mine else plane, :, cols(h)],
            part_send.at[h * PLANES + plane],
            part_recv.at[h * PLANES + (z if mine else plane)],
            along_z(plane),
        )

    def combined(plane, h):
        weight = jnp.where(token_f32 == meta[plane, 0:1, :], meta[plane, 1:2, :], 0.0)
        high = weight.astype(BF16)
        low = (weight - high.astype(F32)).astype(BF16)
        arrived = back[plane, :, :, h * span : (h + 1) * span].reshape(slots, span)
        return (
            jnp.dot(high, arrived, preferred_element_type=F32)
            + jnp.dot(low, arrived, preferred_element_type=F32)
        ).astype(BF16)

    def wait_back(plane, h):
        for d in range(1, EXPERTS):
            back_copy(plane, lax.rem(rank + d, EXPERTS), h, False).wait_recv()

    def hand_copy(h):
        return remote(
            layer_out.at[:, cols(h)],
            out.at[:, cols(h)],
            hand_send.at[h],
            hand_recv.at[h],
            me,
            after,
        )

    for h in range(COLUMN_PARTS):
        lo, hi = h * span, (h + 1) * span

        def combine(i, carry, h=h, lo=lo, hi=hi):
            plane = lax.rem(z + i, PLANES)
            wait_back(plane, h)
            part[plane, :, lo:hi] = combined(plane, h)
            part_copy(plane, h, True).start()
            return carry

        lax.fori_loop(1, PLANES, combine, 0)
        wait_back(z, h)
        home[z, :, lo:hi] = combined(z, h)

    for h in range(COLUMN_PARTS):
        lo, hi = h * span, (h + 1) * span
        for i in range(1, PLANES):
            part_copy(lax.rem(z + i, PLANES), h, False).wait_recv()
        total = home[0, :, lo:hi].astype(F32)
        for p in range(1, PLANES):
            total = total + home[p, :, lo:hi].astype(F32)
        layer_out[:, lo:hi] = (hidden[:, lo:hi].astype(F32) + total).astype(BF16)
        hand_copy(h).start()

    send_gate_up.wait_send()
    send_down.wait_send()

    def sent(i, carry):
        plane = lax.rem(z + i, PLANES)
        for d in range(1, EXPERTS):
            e = lax.rem(rank + d, EXPERTS)
            remote(
                sorted_rows.at[plane, e],
                rows.at[plane, rank],
                go_send.at[plane * EXPERTS + e],
                go_recv.at[plane * EXPERTS + rank],
                in_plane(e),
            ).wait_send()
            for h in range(COLUMN_PARTS):
                back_copy(plane, e, h, True).wait_send()
        return carry

    lax.fori_loop(0, PLANES, sent, 0)
    for i in range(1, PLANES):
        to = lax.rem(z + i, PLANES)
        remote(meta.at[z], meta.at[z], meta_send.at[to], meta_recv.at[z], along_z(to)).wait_send()
        remote(raw.at[z], raw.at[z], raw_send.at[to], raw_recv.at[z], along_z(to)).wait_send()
        for h in range(COLUMN_PARTS):
            part_copy(to, h, True).wait_send()
    for h in range(COLUMN_PARTS):
        hand_copy(h).wait()


def local(hidden_rows, norm_gain, routes, gates, w_gate_up, w_down):
    hidden = hidden_rows[0]
    tokens, width = hidden.shape
    picks = routes.shape[2]
    cap = tokens * picks // EXPERTS
    inner = w_down.shape[2]
    vmem = pl.BlockSpec(memory_space=pltpu.VMEM)
    anywhere = pl.BlockSpec(memory_space=pl.ANY)
    dma = pltpu.SemaphoreType.DMA
    blocks = pltpu.VMEM((PLANES, EXPERTS, cap, width), BF16)
    per_plane = pltpu.VMEM((PLANES, tokens, width), BF16)
    handoff = pl.pallas_call(
        layer_kernel,
        out_shape=jax.ShapeDtypeStruct((tokens, width), BF16),
        in_specs=[vmem] * 4 + [anywhere] * 2,
        out_specs=anywhere,
        scratch_shapes=[
            per_plane,
            pltpu.VMEM((PLANES, 8, EXPERTS * cap), F32),
            blocks,
            blocks,
            pltpu.VMEM((2, width, 2 * inner), BF16),
            pltpu.VMEM((2 * inner, width), BF16),
            pltpu.VMEM((PLANES, EXPERTS * cap, 2 * inner), BF16),
            blocks,
            blocks,
            per_plane,
            per_plane,
            pltpu.VMEM((tokens, width), BF16),
            dma((2,)),
            dma((2,)),
            dma((2,)),
            dma((PLANES,)),
            dma((PLANES,)),
            dma((PLANES,)),
            dma((PLANES,)),
            dma((PLANES * EXPERTS,)),
            dma((PLANES * EXPERTS,)),
            dma((COLUMN_PARTS * PLANES * EXPERTS,)),
            dma((COLUMN_PARTS * PLANES * EXPERTS,)),
            dma((COLUMN_PARTS * PLANES,)),
            dma((COLUMN_PARTS * PLANES,)),
            dma((COLUMN_PARTS,)),
            dma((COLUMN_PARTS,)),
        ],
        compiler_params=pltpu.CompilerParams(
            collective_id=0, has_side_effects=True, vmem_limit_bytes=48 * 1024 * 1024
        ),
        cost_estimate=pl.CostEstimate(
            flops=6 * EXPERTS * SHARDS * cap * width * inner,
            bytes_accessed=2 * (tokens * width * 2 + 3 * width * inner),
            transcendentals=EXPERTS * SHARDS * cap * inner,
        ),
    )(hidden, norm_gain, routes[0], gates[0], w_gate_up[0, 0], w_down[0, 0])
    return handoff[None]


def solution(mesh):
    in_specs = (
        P("section", "expert", None),
        P("section", None),
        P("section", "expert", None),
        P("section", "expert", None),
        P("section", "expert", None, None),
        P("section", "expert", None, None),
    )
    out_specs = P("section", "expert", None)
    return jax.shard_map(local, mesh=mesh, in_specs=in_specs, out_specs=out_specs, check_vma=False)
```

```python
import jax
import jax.numpy as jnp
from jax import lax
from jax.experimental import pallas as pl
from jax.experimental.pallas import tpu as pltpu
from jax.sharding import PartitionSpec as P

EXPERTS = 8
SHARDS = 8
PLANES = 4
SECTIONS = 8
PIECES = 4
MESH = pl.DeviceIdType.MESH
BF16 = jnp.bfloat16
F32 = jnp.float32


def layer_kernel(
    hidden_hbm,
    gain_hbm,
    routes_hbm,
    gates_hbm,
    w_gate_up,
    w_down,
    out,
    hidden,
    gain,
    routes,
    gates,
    raw,
    meta,
    sorted_rows,
    rows,
    gate_up_w,
    down_w,
    total_gate_up,
    act,
    piece,
    back,
    part,
    home,
    layer_out,
    in_sem,
    gu_send,
    gu_recv,
    wd_send,
    wd_recv,
    up_send,
    dn_send,
    raw_recv,
    meta_send,
    meta_recv,
    go_send,
    go_recv,
    back_send,
    back_recv,
    part_send,
    part_recv,
    hand_send,
    hand_recv,
):
    tokens, width = hidden.shape
    cap = rows.shape[3]
    inner = w_down.shape[0]
    slots = EXPERTS * cap
    span = width // PIECES

    section = lax.axis_index("section")
    me = lax.axis_index("expert")
    z = lax.rem(me, PLANES)
    column = lax.div(me, PLANES)
    y = lax.rem(column, 4)
    rank = lax.div(me, SHARDS)
    y_half, y_odd = lax.div(y, 2), lax.rem(y, 2)
    side = lax.rem(y_half + y_odd, 2)
    partner = (column - y_odd + 1 - y_odd) * PLANES + z
    after = lax.rem(section + 1, SECTIONS)
    before = lax.rem(section + SECTIONS - 1, SECTIONS)
    flip = lax.div(z, 2)
    z_low = z + flip * (PLANES - 1 - 2 * z)

    def in_plane(e):
        half = lax.rem(e, 2)
        return (lax.div(e, 2) * 4 + 2 * half + lax.rem(half + side, 2)) * PLANES + z

    def along_z(plane):
        return column * PLANES + plane

    def other_plane(i):
        low = jnp.where(i - 1 < z_low, i - 1, i)
        return low + flip * (PLANES - 1 - 2 * low)

    def cols(c):
        return pl.ds(pl.multiple_of(c * span, span), span)

    def remote(src, dst, send, recv, to, to_section=None):
        return pltpu.make_async_remote_copy(
            src_ref=src,
            dst_ref=dst,
            send_sem=send,
            recv_sem=recv,
            device_id=(section if to_section is None else to_section, to),
            device_id_type=MESH,
        )

    barrier = pltpu.get_barrier_semaphore()

    def greet(to, to_section):
        pl.semaphore_signal(barrier, inc=1, device_id=(to_section, to), device_id_type=MESH)

    for i in range(1, PLANES):
        greet(along_z(lax.rem(z + i, PLANES)), section)
    for d in range(1, EXPERTS):
        greet(in_plane(lax.rem(rank + d, EXPERTS)), section)
    greet(partner, section)
    greet(me, after)
    greet(me, before)

    own_copies = [
        pltpu.make_async_copy(hidden_hbm, hidden, in_sem.at[0]),
        pltpu.make_async_copy(gain_hbm, gain, in_sem.at[1]),
        pltpu.make_async_copy(routes_hbm, routes, in_sem.at[2]),
        pltpu.make_async_copy(gates_hbm, gates, in_sem.at[3]),
        pltpu.make_async_copy(w_gate_up, gate_up_w.at[0], in_sem.at[4]),
    ]
    for copy in own_copies:
        copy.start()

    def own_down(c):
        return pltpu.make_async_copy(
            w_down.at[:, cols(c)], down_w.at[c, pl.ds(0, inner)], in_sem.at[5 + c]
        )

    for c in range(PIECES):
        own_down(c).start()
    for copy in own_copies[:4]:
        copy.wait()

    rows_f32 = hidden[...].astype(F32)
    scale = lax.rsqrt(jnp.mean(rows_f32 * rows_f32, axis=1, keepdims=True) + 1e-06)
    for c in range(PIECES):
        lo, hi = c * span, (c + 1) * span
        raw[c, z] = (hidden[:, lo:hi].astype(F32) * scale * gain[:, lo:hi]).astype(BF16)

    names = lax.broadcasted_iota(jnp.int32, (16, tokens), 0)
    first, second = routes[0:1, :], routes[1:2, :]
    names_first, names_second = names == first, names == second
    one_hot = (jnp.where(names_first, 1.0, 0.0) + jnp.where(names_second, 1.0, 0.0)).astype(BF16)
    above = jnp.where(
        lax.broadcasted_iota(jnp.int32, (tokens, tokens), 0)
        < lax.broadcasted_iota(jnp.int32, (tokens, tokens), 1),
        1.0,
        0.0,
    ).astype(BF16)
    earlier = jnp.dot(one_hot, above, preferred_element_type=F32)
    slot_first = first.astype(F32) * cap + jnp.sum(
        jnp.where(names_first, earlier, 0.0), axis=0, keepdims=True
    )
    slot_second = second.astype(F32) * cap + jnp.sum(
        jnp.where(names_second, earlier, 0.0), axis=0, keepdims=True
    )
    meta_row = lax.broadcasted_iota(jnp.int32, (8, tokens), 0)
    meta[z, :, 0:tokens] = jnp.where(
        meta_row == 0,
        slot_first,
        jnp.where(
            meta_row == 1, slot_second, jnp.where(meta_row == 2, gates[0:1, :], gates[1:2, :])
        ),
    )
    meta[z, :, tokens : 2 * tokens] = jnp.zeros((8, tokens), F32)

    pl.semaphore_wait(barrier, PLANES - 1 + EXPERTS - 1 + 3)

    def gate_up_copy(c):
        return remote(
            w_gate_up.at[pl.ds(pl.multiple_of(c * span, span), span)],
            gate_up_w.at[1, pl.ds(pl.multiple_of(c * span, span), span)],
            gu_send.at[c],
            gu_recv.at[c],
            partner,
        )

    def down_copy(c):
        return remote(
            w_down.at[:, cols(c)],
            down_w.at[c, pl.ds(inner, inner)],
            wd_send.at[c],
            wd_recv.at[c],
            partner,
        )

    def meta_copy(to, plane):
        return remote(
            meta.at[plane], meta.at[plane], meta_send.at[to], meta_recv.at[plane], along_z(to)
        )

    def up_copy(c, plane):
        at = c * PLANES + plane
        return remote(raw.at[c, plane], raw.at[c, plane], up_send.at[at], raw_recv.at[at], me + 1)

    def dn_copy(c, plane):
        at = c * PLANES + plane
        return remote(raw.at[c, plane], raw.at[c, plane], dn_send.at[at], raw_recv.at[at], me - 1)

    def pass_on(c, plane, act_on):
        @pl.when((plane <= z) & (z < PLANES - 1))
        def _():
            act_on(up_copy(c, plane))

        @pl.when((plane >= z) & (z > 0))
        def _():
            act_on(dn_copy(c, plane))

    def go_copy(c, plane, e, mine):
        slot = rank if mine else e
        at = (c * PLANES + plane) * EXPERTS
        return remote(
            sorted_rows.at[c, plane, e],
            rows.at[c, plane, slot],
            go_send.at[at + e],
            go_recv.at[at + slot],
            in_plane(e),
        )

    slot_row = lax.broadcasted_iota(jnp.int32, (slots, tokens), 0).astype(F32)

    def sort_and_send(c, plane):
        placed = (
            jnp.where(slot_row == meta[plane, 0:1, 0:tokens], 1.0, 0.0)
            + jnp.where(slot_row == meta[plane, 1:2, 0:tokens], 1.0, 0.0)
        ).astype(BF16)
        block = jnp.dot(placed, raw[c, plane], preferred_element_type=F32).astype(BF16)
        sorted_rows[c, plane] = block.reshape(EXPERTS, cap, span)
        for d in range(1, EXPERTS):
            go_copy(c, plane, lax.rem(rank + d, EXPERTS), True).start()
        rows[c, plane, rank] = sorted_rows[c, plane, rank]

    for i in range(1, PLANES):
        meta_copy(lax.rem(z + i, PLANES), z).start()
    for c in range(PIECES):
        pass_on(c, z, lambda copy: copy.start())
        gate_up_copy(c).start()

    def own_dispatch(c, carry):
        sort_and_send(c, z)
        return carry

    lax.fori_loop(0, PIECES, own_dispatch, 0)
    for i in range(1, PLANES):
        plane = lax.rem(z + i, PLANES)
        meta_copy(z, plane).wait_recv()

    def dispatch(n, carry):
        c = lax.div(n, PLANES - 1)
        plane = other_plane(lax.rem(n, PLANES - 1) + 1)
        at = c * PLANES + plane
        remote(raw.at[c, plane], raw.at[c, plane], up_send.at[at], raw_recv.at[at], me).wait_recv()
        pass_on(c, plane, lambda copy: copy.start())
        sort_and_send(c, plane)
        return carry

    lax.fori_loop(0, PIECES * (PLANES - 1), dispatch, 0)
    for c in range(PIECES):
        down_copy(c).start()

    own_copies[4].wait()

    def gate_up(c, carry):
        def arrived(plane, carry):
            for d in range(1, EXPERTS):
                go_copy(c, plane, lax.rem(rank + d, EXPERTS), False).wait_recv()
            return carry

        lax.fori_loop(0, PLANES, arrived, 0)
        gate_up_copy(c).wait_recv()
        block = rows[c].reshape(PLANES * slots, span)
        for s in range(2):
            w = gate_up_w[s, pl.ds(pl.multiple_of(c * span, span), span), :]
            total_gate_up[s] = total_gate_up[s] + jnp.dot(block, w, preferred_element_type=F32)
        return carry

    total_gate_up[...] = jnp.zeros_like(total_gate_up)
    lax.fori_loop(0, PIECES, gate_up, 0)
    for s in range(2):
        gate = total_gate_up[s, :, 0:inner]
        act[:, s * inner : (s + 1) * inner] = (
            gate / (1.0 + jnp.exp(-gate)) * total_gate_up[s, :, inner : 2 * inner]
        ).astype(BF16)

    def back_copy(c, plane, e, mine):
        slot = rank if mine else e
        at = (c * PLANES + plane) * EXPERTS
        return remote(
            piece.at[c, plane, e],
            back.at[c, plane, slot],
            back_send.at[at + e],
            back_recv.at[at + slot],
            in_plane(e),
        )

    def down(c, carry):
        own_down(c).wait()
        down_copy(c).wait_recv()
        block = jnp.dot(act[...], down_w[c], preferred_element_type=F32).astype(BF16)
        piece[c] = block.reshape(PLANES, EXPERTS, cap, span)

        def send(i, carry):
            plane = jnp.where(i == PLANES, z, other_plane(PLANES - i))
            for d in range(1, EXPERTS):
                back_copy(c, plane, lax.rem(rank + d, EXPERTS), True).start()
            back[c, plane, rank] = piece[c, plane, rank]
            return carry

        lax.fori_loop(1, PLANES + 1, send, 0)
        return carry

    lax.fori_loop(0, PIECES, down, 0)

    def part_copy(c, plane, mine):
        slot = z if mine else plane
        return remote(
            part.at[c, plane],
            home.at[c, slot],
            part_send.at[c * PLANES + plane],
            part_recv.at[c * PLANES + slot],
            along_z(plane),
        )

    def combined(c, plane):
        for d in range(1, EXPERTS):
            back_copy(c, plane, lax.rem(rank + d, EXPERTS), False).wait_recv()
        weight = jnp.where(
            slot_row == meta[plane, 0:1, 0:tokens], meta[plane, 2:3, 0:tokens], 0.0
        ) + jnp.where(slot_row == meta[plane, 1:2, 0:tokens], meta[plane, 3:4, 0:tokens], 0.0)
        high = weight.astype(BF16)
        low = (weight - high.astype(F32)).astype(BF16)
        both = lax.dot_general(
            jnp.concatenate([high, low], axis=1),
            back[c, plane].reshape(slots, span),
            (((0,), (0,)), ((), ())),
            preferred_element_type=F32,
        )
        return (both[0:tokens] + both[tokens : 2 * tokens]).astype(BF16)

    def hand_copy(c):
        return remote(
            layer_out.at[c], out.at[:, cols(c)], hand_send.at[c], hand_recv.at[c], me, after
        )

    def combine(c):
        def send(i, carry):
            plane = other_plane(PLANES - i)
            part[c, plane] = combined(c, plane)
            part_copy(c, plane, True).start()
            return carry

        lax.fori_loop(1, PLANES, send, 0)
        home[c, z] = combined(c, z)

    def finish(c):
        for i in range(1, PLANES):
            part_copy(c, lax.rem(z + i, PLANES), False).wait_recv()
        total = home[c, 0].astype(F32)
        for p in range(1, PLANES):
            total = total + home[c, p].astype(F32)
        layer_out[c] = (hidden[:, cols(c)].astype(F32) + total).astype(BF16)
        hand_copy(c).start()

    def combine_and_finish(c, carry):
        combine(c)
        finish(c - 1)
        return carry

    combine(0)
    lax.fori_loop(1, PIECES, combine_and_finish, 0)
    finish(PIECES - 1)

    def sent(c, carry):
        gate_up_copy(c).wait_send()
        down_copy(c).wait_send()

        def sent_plane(plane, carry):
            for d in range(1, EXPERTS):
                e = lax.rem(rank + d, EXPERTS)
                go_copy(c, plane, e, True).wait_send()
                back_copy(c, plane, e, True).wait_send()
            pass_on(c, plane, lambda copy: copy.wait_send())
            return carry

        lax.fori_loop(0, PLANES, sent_plane, 0)
        for i in range(1, PLANES):
            part_copy(c, lax.rem(z + i, PLANES), True).wait_send()
        return carry

    lax.fori_loop(0, PIECES, sent, 0)
    for i in range(1, PLANES):
        meta_copy(lax.rem(z + i, PLANES), z).wait_send()
    for c in range(PIECES):
        hand_copy(c).wait()


def local(hidden_rows, norm_gain, routes, gates, w_gate_up, w_down):
    hidden = hidden_rows[0]
    tokens, width = hidden.shape
    picks = routes.shape[2]
    cap = tokens * picks // EXPERTS
    inner = w_down.shape[2]
    span = width // PIECES
    slots = EXPERTS * cap
    hbm = pl.BlockSpec(memory_space=pltpu.HBM)
    dma = pltpu.SemaphoreType.DMA
    blocks = pltpu.VMEM((PIECES, PLANES, EXPERTS, cap, span), BF16)
    per_plane = pltpu.VMEM((PIECES, PLANES, tokens, span), BF16)
    handoff = pl.pallas_call(
        layer_kernel,
        out_shape=jax.ShapeDtypeStruct((tokens, width), BF16),
        in_specs=[hbm] * 6,
        out_specs=hbm,
        scratch_shapes=[
            pltpu.VMEM((tokens, width), BF16),
            pltpu.VMEM((1, width), F32),
            pltpu.VMEM((picks, tokens), jnp.int32),
            pltpu.VMEM((picks, tokens), F32),
            per_plane,
            pltpu.VMEM((PLANES, 8, 2 * tokens), F32),
            blocks,
            blocks,
            pltpu.VMEM((2, width, 2 * inner), BF16),
            pltpu.VMEM((PIECES, 2 * inner, span), BF16),
            pltpu.VMEM((2, PLANES * slots, 2 * inner), F32),
            pltpu.VMEM((PLANES * slots, 2 * inner), BF16),
            blocks,
            blocks,
            per_plane,
            per_plane,
            pltpu.VMEM((PIECES, tokens, span), BF16),
            dma((5 + PIECES,)),
            dma((PIECES,)),
            dma((PIECES,)),
            dma((PIECES,)),
            dma((PIECES,)),
            dma((PIECES * PLANES,)),
            dma((PIECES * PLANES,)),
            dma((PIECES * PLANES,)),
            dma((PLANES,)),
            dma((PLANES,)),
            dma((PIECES * PLANES * EXPERTS,)),
            dma((PIECES * PLANES * EXPERTS,)),
            dma((PIECES * PLANES * EXPERTS,)),
            dma((PIECES * PLANES * EXPERTS,)),
            dma((PIECES * PLANES,)),
            dma((PIECES * PLANES,)),
            dma((PIECES,)),
            dma((PIECES,)),
        ],
        compiler_params=pltpu.CompilerParams(
            collective_id=0, has_side_effects=True, vmem_limit_bytes=62 * 1024 * 1024
        ),
        cost_estimate=pl.CostEstimate(
            flops=6 * EXPERTS * SHARDS * cap * width * inner,
            bytes_accessed=2 * (tokens * width * 2 + 3 * width * inner),
            transcendentals=EXPERTS * SHARDS * cap * inner,
        ),
    )(hidden, norm_gain, routes[0].T, gates[0].T, w_gate_up[0, 0], w_down[0, 0])
    return handoff[None]


def solution(mesh):
    in_specs = (
        P("section", "expert", None),
        P("section", None),
        P("section", "expert", None),
        P("section", "expert", None),
        P("section", "expert", None, None),
        P("section", "expert", None, None),
    )
    out_specs = P("section", "expert", None)
    return jax.shard_map(local, mesh=mesh, in_specs=in_specs, out_specs=out_specs, check_vma=False)
```

```python
import jax
import jax.numpy as jnp
from jax import lax
from jax.experimental import pallas as pl
from jax.experimental.pallas import tpu as pltpu
from jax.sharding import PartitionSpec as P

EXPERTS = 8
SHARDS = 8
PLANES = 4
SECTIONS = 8
PIECES = 4
BACK_PIECES = 7
AHEAD = 2
MESH = pl.DeviceIdType.MESH
BF16 = jnp.bfloat16
F32 = jnp.float32


def layer_kernel(
    hidden_hbm,
    gain_hbm,
    routes_hbm,
    gates_hbm,
    w_gate_up,
    w_down,
    out,
    hidden,
    gain,
    routes,
    gates,
    raw,
    meta,
    sorted_rows,
    rows,
    gate_up_w,
    down_w,
    total_gate_up,
    act,
    piece,
    back,
    part,
    from_below,
    from_above,
    total_part,
    home,
    layer_out,
    in_sem,
    gu_send,
    gu_recv,
    wd_send,
    wd_recv,
    up_send,
    dn_send,
    raw_recv,
    meta_send,
    meta_recv,
    go_send,
    go_recv,
    back_send,
    back_recv,
    part_send,
    below_recv,
    above_recv,
    hand_send,
    hand_recv,
):
    tokens, width = hidden.shape
    cap = rows.shape[3]
    inner = w_down.shape[0]
    slots = EXPERTS * cap
    span = width // PIECES
    back_span = width // BACK_PIECES

    section = lax.axis_index("section")
    me = lax.axis_index("expert")
    z = lax.rem(me, PLANES)
    column = lax.div(me, PLANES)
    y = lax.rem(column, 4)
    rank = lax.div(me, SHARDS)
    y_half, y_odd = lax.div(y, 2), lax.rem(y, 2)
    side = lax.rem(y_half + y_odd, 2)
    partner = (column - y_odd + 1 - y_odd) * PLANES + z
    after = lax.rem(section + 1, SECTIONS)
    before = lax.rem(section + SECTIONS - 1, SECTIONS)
    flip = lax.div(z, 2)
    z_low = z + flip * (PLANES - 1 - 2 * z)

    def in_plane(e):
        half = lax.rem(e, 2)
        return (lax.div(e, 2) * 4 + 2 * half + lax.rem(half + side, 2)) * PLANES + z

    def along_z(plane):
        return column * PLANES + plane

    def other_plane(i):
        low = jnp.where(i - 1 < z_low, i - 1, i)
        return low + flip * (PLANES - 1 - 2 * low)

    def cols(c):
        return pl.ds(pl.multiple_of(c * back_span, back_span), back_span)

    def remote(src, dst, send, recv, to, to_section=None):
        return pltpu.make_async_remote_copy(
            src_ref=src,
            dst_ref=dst,
            send_sem=send,
            recv_sem=recv,
            device_id=(section if to_section is None else to_section, to),
            device_id_type=MESH,
        )

    barrier = pltpu.get_barrier_semaphore()

    def greet(to, to_section):
        pl.semaphore_signal(barrier, inc=1, device_id=(to_section, to), device_id_type=MESH)

    for i in range(1, PLANES):
        greet(along_z(lax.rem(z + i, PLANES)), section)
    for d in range(1, EXPERTS):
        greet(in_plane(lax.rem(rank + d, EXPERTS)), section)
    greet(partner, section)
    greet(me, before)

    own_copies = [
        pltpu.make_async_copy(hidden_hbm, hidden, in_sem.at[0]),
        pltpu.make_async_copy(gain_hbm, gain, in_sem.at[1]),
        pltpu.make_async_copy(routes_hbm, routes, in_sem.at[2]),
        pltpu.make_async_copy(gates_hbm, gates, in_sem.at[3]),
        pltpu.make_async_copy(w_gate_up, gate_up_w.at[0], in_sem.at[4]),
    ]
    for copy in own_copies:
        copy.start()

    def own_down(c):
        return pltpu.make_async_copy(
            w_down.at[:, cols(c)], down_w.at[c, pl.ds(0, inner)], in_sem.at[5 + c]
        )

    for c in range(BACK_PIECES):
        own_down(c).start()
    for copy in own_copies[:4]:
        copy.wait()

    rows_f32 = hidden[...].astype(F32)
    scale = lax.rsqrt(jnp.mean(rows_f32 * rows_f32, axis=1, keepdims=True) + 1e-06)
    for c in range(PIECES):
        lo, hi = c * span, (c + 1) * span
        raw[c, z] = (hidden[:, lo:hi].astype(F32) * scale * gain[:, lo:hi]).astype(BF16)

    names = lax.broadcasted_iota(jnp.int32, (16, tokens), 0)
    first, second = routes[0:1, :], routes[1:2, :]
    names_first, names_second = names == first, names == second
    one_hot = (jnp.where(names_first, 1.0, 0.0) + jnp.where(names_second, 1.0, 0.0)).astype(BF16)
    above = jnp.where(
        lax.broadcasted_iota(jnp.int32, (tokens, tokens), 0)
        < lax.broadcasted_iota(jnp.int32, (tokens, tokens), 1),
        1.0,
        0.0,
    ).astype(BF16)
    earlier = jnp.dot(one_hot, above, preferred_element_type=F32)
    slot_first = first.astype(F32) * cap + jnp.sum(
        jnp.where(names_first, earlier, 0.0), axis=0, keepdims=True
    )
    slot_second = second.astype(F32) * cap + jnp.sum(
        jnp.where(names_second, earlier, 0.0), axis=0, keepdims=True
    )
    meta_row = lax.broadcasted_iota(jnp.int32, (8, tokens), 0)
    meta[z, :, 0:tokens] = jnp.where(
        meta_row == 0,
        slot_first,
        jnp.where(
            meta_row == 1, slot_second, jnp.where(meta_row == 2, gates[0:1, :], gates[1:2, :])
        ),
    )
    meta[z, :, tokens : 2 * tokens] = jnp.zeros((8, tokens), F32)

    pl.semaphore_wait(barrier, PLANES - 1 + EXPERTS - 1 + 2)

    def gate_up_copy(c):
        return remote(
            w_gate_up.at[pl.ds(pl.multiple_of(c * span, span), span)],
            gate_up_w.at[1, pl.ds(pl.multiple_of(c * span, span), span)],
            gu_send.at[c],
            gu_recv.at[c],
            partner,
        )

    def down_copy(c):
        return remote(
            w_down.at[:, cols(c)],
            down_w.at[c, pl.ds(inner, inner)],
            wd_send.at[c],
            wd_recv.at[c],
            partner,
        )

    def meta_copy(to, plane):
        return remote(
            meta.at[plane], meta.at[plane], meta_send.at[to], meta_recv.at[plane], along_z(to)
        )

    def up_copy(c, plane):
        at = c * PLANES + plane
        return remote(raw.at[c, plane], raw.at[c, plane], up_send.at[at], raw_recv.at[at], me + 1)

    def dn_copy(c, plane):
        at = c * PLANES + plane
        return remote(raw.at[c, plane], raw.at[c, plane], dn_send.at[at], raw_recv.at[at], me - 1)

    def pass_on(c, plane, act_on):
        @pl.when((plane <= z) & (z < PLANES - 1))
        def _():
            act_on(up_copy(c, plane))

        @pl.when((plane >= z) & (z > 0))
        def _():
            act_on(dn_copy(c, plane))

    def go_copy(c, plane, e, mine):
        slot = rank if mine else e
        at = (c * PLANES + plane) * EXPERTS
        return remote(
            sorted_rows.at[c, plane, e],
            rows.at[c, plane, slot],
            go_send.at[at + e],
            go_recv.at[at + slot],
            in_plane(e),
        )

    slot_row = lax.broadcasted_iota(jnp.int32, (slots, tokens), 0).astype(F32)

    def sort_and_send(c, plane):
        placed = (
            jnp.where(slot_row == meta[plane, 0:1, 0:tokens], 1.0, 0.0)
            + jnp.where(slot_row == meta[plane, 1:2, 0:tokens], 1.0, 0.0)
        ).astype(BF16)
        block = jnp.dot(placed, raw[c, plane], preferred_element_type=F32).astype(BF16)
        sorted_rows[c, plane] = block.reshape(EXPERTS, cap, span)
        for d in range(1, EXPERTS):
            go_copy(c, plane, lax.rem(rank + d, EXPERTS), True).start()
        rows[c, plane, rank] = sorted_rows[c, plane, rank]

    for i in range(1, PLANES):
        meta_copy(lax.rem(z + i, PLANES), z).start()
    for c in range(PIECES):
        pass_on(c, z, lambda copy: copy.start())
        gate_up_copy(c).start()

    def own_dispatch(c, carry):
        sort_and_send(c, z)
        return carry

    lax.fori_loop(0, PIECES, own_dispatch, 0)
    for i in range(1, PLANES):
        plane = lax.rem(z + i, PLANES)
        meta_copy(z, plane).wait_recv()

    def dispatch(n, carry):
        c = lax.div(n, PLANES - 1)
        plane = other_plane(lax.rem(n, PLANES - 1) + 1)
        at = c * PLANES + plane
        remote(raw.at[c, plane], raw.at[c, plane], up_send.at[at], raw_recv.at[at], me).wait_recv()
        pass_on(c, plane, lambda copy: copy.start())
        sort_and_send(c, plane)
        return carry

    lax.fori_loop(0, PIECES * (PLANES - 1), dispatch, 0)
    for c in range(BACK_PIECES):
        down_copy(c).start()

    own_copies[4].wait()

    def gate_up(c, carry):
        def arrived(plane, carry):
            for d in range(1, EXPERTS):
                go_copy(c, plane, lax.rem(rank + d, EXPERTS), False).wait_recv()
            return carry

        lax.fori_loop(0, PLANES, arrived, 0)
        gate_up_copy(c).wait_recv()
        block = rows[c].reshape(PLANES * slots, span)
        for s in range(2):
            w = gate_up_w[s, pl.ds(pl.multiple_of(c * span, span), span), :]
            total_gate_up[s] = total_gate_up[s] + jnp.dot(block, w, preferred_element_type=F32)
        return carry

    total_gate_up[...] = jnp.zeros_like(total_gate_up)
    lax.fori_loop(0, PIECES, gate_up, 0)
    for s in range(2):
        gate = total_gate_up[s, :, 0:inner]
        act[:, s * inner : (s + 1) * inner] = (
            gate / (1.0 + jnp.exp(-gate)) * total_gate_up[s, :, inner : 2 * inner]
        ).astype(BF16)

    def back_copy(c, plane, e, mine):
        slot = rank if mine else e
        at = (c * PLANES + plane) * EXPERTS
        return remote(
            piece.at[c, plane, e],
            back.at[c, plane, slot],
            back_send.at[at + e],
            back_recv.at[at + slot],
            in_plane(e),
        )

    def down(c):
        own_down(c).wait()
        down_copy(c).wait_recv()
        block = jnp.dot(act[...], down_w[c], preferred_element_type=F32).astype(BF16)
        piece[c] = block.reshape(PLANES, EXPERTS, cap, back_span)

        def send(i, carry):
            plane = jnp.where(i == PLANES, z, other_plane(PLANES - i))
            for d in range(1, EXPERTS):
                back_copy(c, plane, lax.rem(rank + d, EXPERTS), True).start()
            back[c, plane, rank] = piece[c, plane, rank]
            return carry

        lax.fori_loop(1, PLANES + 1, send, 0)

    def part_up(c, plane):
        at = c * PLANES + plane
        return remote(
            part.at[c, plane], from_below.at[c, plane], part_send.at[at], below_recv.at[at], me + 1
        )

    def part_down(c, plane):
        at = c * PLANES + plane
        return remote(
            part.at[c, plane], from_above.at[c, plane], part_send.at[at], above_recv.at[at], me - 1
        )

    def combined(c, plane):
        for d in range(1, EXPERTS):
            back_copy(c, plane, lax.rem(rank + d, EXPERTS), False).wait_recv()
        weight = jnp.where(
            slot_row == meta[plane, 0:1, 0:tokens], meta[plane, 2:3, 0:tokens], 0.0
        ) + jnp.where(slot_row == meta[plane, 1:2, 0:tokens], meta[plane, 3:4, 0:tokens], 0.0)
        high = weight.astype(BF16)
        low = (weight - high.astype(F32)).astype(BF16)
        both = lax.dot_general(
            jnp.concatenate([high, low], axis=1),
            back[c, plane].reshape(slots, back_span),
            (((0,), (0,)), ((), ())),
            preferred_element_type=F32,
        )
        return both[0:tokens] + both[tokens : 2 * tokens]

    def hand_copy(c):
        return remote(
            layer_out.at[c], out.at[:, cols(c)], hand_send.at[c], hand_recv.at[c], me, after
        )

    def combine(c):
        def send(i, carry):
            plane = other_plane(PLANES - i)
            total_part[...] = combined(c, plane)

            @pl.when((plane > z) & (z > 0))
            def _():
                part_up(c, plane).wait_recv()
                total_part[...] += from_below[c, plane].astype(F32)

            @pl.when((plane < z) & (z < PLANES - 1))
            def _():
                part_down(c, plane).wait_recv()
                total_part[...] += from_above[c, plane].astype(F32)

            part[c, plane] = total_part[...].astype(BF16)

            @pl.when(plane > z)
            def _():
                part_up(c, plane).start()

            @pl.when(plane < z)
            def _():
                part_down(c, plane).start()

            return carry

        lax.fori_loop(1, PLANES, send, 0)
        home[c] = hidden[:, cols(c)].astype(F32) + combined(c, z)

    def finish(c):
        @pl.when(z > 0)
        def _():
            part_up(c, z).wait_recv()
            home[c] += from_below[c, z].astype(F32)

        @pl.when(z < PLANES - 1)
        def _():
            part_down(c, z).wait_recv()
            home[c] += from_above[c, z].astype(F32)

        layer_out[c] = home[c].astype(BF16)
        hand_copy(c).start()

    def way_back(c, carry):
        @pl.when(c + AHEAD < BACK_PIECES)
        def _():
            down(c + AHEAD)

        combine(c)

        @pl.when(c > 0)
        def _():
            finish(c - 1)

        return carry

    for c in range(AHEAD):
        down(c)
    lax.fori_loop(0, BACK_PIECES, way_back, 0)
    finish(BACK_PIECES - 1)

    def sent(c, carry):
        gate_up_copy(c).wait_send()

        def sent_plane(plane, carry):
            for d in range(1, EXPERTS):
                go_copy(c, plane, lax.rem(rank + d, EXPERTS), True).wait_send()
            pass_on(c, plane, lambda copy: copy.wait_send())
            return carry

        lax.fori_loop(0, PLANES, sent_plane, 0)
        return carry

    def sent_back(c, carry):
        down_copy(c).wait_send()

        def sent_plane(plane, carry):
            for d in range(1, EXPERTS):
                back_copy(c, plane, lax.rem(rank + d, EXPERTS), True).wait_send()
            return carry

        lax.fori_loop(0, PLANES, sent_plane, 0)
        for i in range(1, PLANES):
            part_up(c, lax.rem(z + i, PLANES)).wait_send()
        return carry

    lax.fori_loop(0, PIECES, sent, 0)
    lax.fori_loop(0, BACK_PIECES, sent_back, 0)
    for i in range(1, PLANES):
        meta_copy(lax.rem(z + i, PLANES), z).wait_send()
    for c in range(BACK_PIECES):
        hand_copy(c).wait()


def local(hidden_rows, norm_gain, routes, gates, w_gate_up, w_down):
    hidden = hidden_rows[0]
    tokens, width = hidden.shape
    picks = routes.shape[2]
    cap = tokens * picks // EXPERTS
    inner = w_down.shape[2]
    span = width // PIECES
    back_span = width // BACK_PIECES
    slots = EXPERTS * cap
    hbm = pl.BlockSpec(memory_space=pltpu.HBM)
    dma = pltpu.SemaphoreType.DMA
    blocks = pltpu.VMEM((PIECES, PLANES, EXPERTS, cap, span), BF16)
    per_plane = pltpu.VMEM((PIECES, PLANES, tokens, span), BF16)
    back_blocks = pltpu.VMEM((BACK_PIECES, PLANES, EXPERTS, cap, back_span), BF16)
    back_per_plane = pltpu.VMEM((BACK_PIECES, PLANES, tokens, back_span), BF16)
    handoff = pl.pallas_call(
        layer_kernel,
        out_shape=jax.ShapeDtypeStruct((tokens, width), BF16),
        in_specs=[hbm] * 6,
        out_specs=hbm,
        scratch_shapes=[
            pltpu.VMEM((tokens, width), BF16),
            pltpu.VMEM((1, width), F32),
            pltpu.VMEM((picks, tokens), jnp.int32),
            pltpu.VMEM((picks, tokens), F32),
            per_plane,
            pltpu.VMEM((PLANES, 8, 2 * tokens), F32),
            blocks,
            blocks,
            pltpu.VMEM((2, width, 2 * inner), BF16),
            pltpu.VMEM((BACK_PIECES, 2 * inner, back_span), BF16),
            pltpu.VMEM((2, PLANES * slots, 2 * inner), F32),
            pltpu.VMEM((PLANES * slots, 2 * inner), BF16),
            back_blocks,
            back_blocks,
            back_per_plane,
            back_per_plane,
            back_per_plane,
            pltpu.VMEM((tokens, back_span), F32),
            pltpu.VMEM((BACK_PIECES, tokens, back_span), F32),
            pltpu.VMEM((BACK_PIECES, tokens, back_span), BF16),
            dma((5 + BACK_PIECES,)),
            dma((PIECES,)),
            dma((PIECES,)),
            dma((BACK_PIECES,)),
            dma((BACK_PIECES,)),
            dma((PIECES * PLANES,)),
            dma((PIECES * PLANES,)),
            dma((PIECES * PLANES,)),
            dma((PLANES,)),
            dma((PLANES,)),
            dma((PIECES * PLANES * EXPERTS,)),
            dma((PIECES * PLANES * EXPERTS,)),
            dma((BACK_PIECES * PLANES * EXPERTS,)),
            dma((BACK_PIECES * PLANES * EXPERTS,)),
            dma((BACK_PIECES * PLANES,)),
            dma((BACK_PIECES * PLANES,)),
            dma((BACK_PIECES * PLANES,)),
            dma((BACK_PIECES,)),
            dma((BACK_PIECES,)),
        ],
        compiler_params=pltpu.CompilerParams(
            collective_id=0, has_side_effects=True, vmem_limit_bytes=62 * 1024 * 1024
        ),
        cost_estimate=pl.CostEstimate(
            flops=6 * EXPERTS * SHARDS * cap * width * inner,
            bytes_accessed=2 * (tokens * width * 2 + 3 * width * inner),
            transcendentals=EXPERTS * SHARDS * cap * inner,
        ),
    )(hidden, norm_gain, routes[0].T, gates[0].T, w_gate_up[0, 0], w_down[0, 0])
    return handoff[None]


def solution(mesh):
    in_specs = (
        P("section", "expert", None),
        P("section", None),
        P("section", "expert", None),
        P("section", "expert", None),
        P("section", "expert", None, None),
        P("section", "expert", None, None),
    )
    out_specs = P("section", "expert", None)
    return jax.shard_map(local, mesh=mesh, in_specs=in_specs, out_specs=out_specs, check_vma=False)
```

```python
import jax
import jax.numpy as jnp
from jax import lax
from jax.experimental import pallas as pl
from jax.experimental.pallas import tpu as pltpu
from jax.sharding import PartitionSpec as P

EXPERTS = 8
SHARDS = 8
PLANES = 4
SECTIONS = 8
PIECES = 4
BACK_PIECES = 7
AHEAD = 2
DOWN_AHEAD = 3
MESH = pl.DeviceIdType.MESH
BF16 = jnp.bfloat16
F32 = jnp.float32


def layer_kernel(
    hidden_hbm,
    gain_hbm,
    routes_hbm,
    gates_hbm,
    w_gate_up,
    w_down,
    out,
    hidden,
    gain,
    routes,
    gates,
    raw,
    meta,
    sorted_rows,
    rows,
    gate_up_w,
    down_w,
    total_gate_up,
    act,
    piece,
    back,
    part,
    from_below,
    from_above,
    total_part,
    home,
    layer_out,
    in_sem,
    gu_send,
    gu_recv,
    wd_send,
    wd_recv,
    up_send,
    dn_send,
    raw_recv,
    meta_send,
    meta_recv,
    go_send,
    go_recv,
    back_send,
    back_recv,
    part_send,
    below_recv,
    above_recv,
    hand_send,
    hand_recv,
):
    tokens, width = hidden.shape
    cap = rows.shape[3]
    inner = w_down.shape[0]
    slots = EXPERTS * cap
    span = width // PIECES
    back_span = width // BACK_PIECES

    section = lax.axis_index("section")
    me = lax.axis_index("expert")
    z = lax.rem(me, PLANES)
    column = lax.div(me, PLANES)
    y = lax.rem(column, 4)
    rank = lax.div(me, SHARDS)
    y_half, y_odd = lax.div(y, 2), lax.rem(y, 2)
    side = lax.rem(y_half + y_odd, 2)
    partner = (column - y_odd + 1 - y_odd) * PLANES + z
    after = lax.rem(section + 1, SECTIONS)
    before = lax.rem(section + SECTIONS - 1, SECTIONS)
    flip = lax.div(z, 2)
    z_low = z + flip * (PLANES - 1 - 2 * z)

    def in_plane(e):
        half = lax.rem(e, 2)
        return (lax.div(e, 2) * 4 + 2 * half + lax.rem(half + side, 2)) * PLANES + z

    def along_z(plane):
        return column * PLANES + plane

    def other_plane(i):
        low = jnp.where(i - 1 < z_low, i - 1, i)
        return low + flip * (PLANES - 1 - 2 * low)

    def cols(c):
        return pl.ds(pl.multiple_of(c * back_span, back_span), back_span)

    def remote(src, dst, send, recv, to, to_section=None):
        return pltpu.make_async_remote_copy(
            src_ref=src,
            dst_ref=dst,
            send_sem=send,
            recv_sem=recv,
            device_id=(section if to_section is None else to_section, to),
            device_id_type=MESH,
        )

    others = [lax.rem(rank + d, EXPERTS) for d in range(1, EXPERTS)]
    plane_peers = [(e, in_plane(e)) for e in others]

    barrier = pltpu.get_barrier_semaphore()

    def greet(to, to_section):
        pl.semaphore_signal(barrier, inc=1, device_id=(to_section, to), device_id_type=MESH)

    for i in range(1, PLANES):
        greet(along_z(lax.rem(z + i, PLANES)), section)
    for _, to in plane_peers:
        greet(to, section)
    greet(partner, section)
    greet(me, before)

    own_copies = [
        pltpu.make_async_copy(hidden_hbm, hidden, in_sem.at[0]),
        pltpu.make_async_copy(gain_hbm, gain, in_sem.at[1]),
        pltpu.make_async_copy(routes_hbm, routes, in_sem.at[2]),
        pltpu.make_async_copy(gates_hbm, gates, in_sem.at[3]),
        pltpu.make_async_copy(w_gate_up, gate_up_w.at[0], in_sem.at[4]),
    ]
    for copy in own_copies:
        copy.start()

    def own_down(c):
        return pltpu.make_async_copy(
            w_down.at[:, cols(c)], down_w.at[c, pl.ds(0, inner)], in_sem.at[5 + c]
        )

    for c in range(BACK_PIECES):
        own_down(c).start()
    for copy in own_copies[:4]:
        copy.wait()

    rows_f32 = hidden[...].astype(F32)
    scale = lax.rsqrt(jnp.mean(rows_f32 * rows_f32, axis=1, keepdims=True) + 1e-06)
    for c in range(PIECES):
        lo, hi = c * span, (c + 1) * span
        raw[c, z] = (hidden[:, lo:hi].astype(F32) * scale * gain[:, lo:hi]).astype(BF16)

    names = lax.broadcasted_iota(jnp.int32, (16, tokens), 0)
    first, second = routes[0:1, :], routes[1:2, :]
    names_first, names_second = names == first, names == second
    one_hot = (jnp.where(names_first, 1.0, 0.0) + jnp.where(names_second, 1.0, 0.0)).astype(BF16)
    above = jnp.where(
        lax.broadcasted_iota(jnp.int32, (tokens, tokens), 0)
        < lax.broadcasted_iota(jnp.int32, (tokens, tokens), 1),
        1.0,
        0.0,
    ).astype(BF16)
    earlier = jnp.dot(one_hot, above, preferred_element_type=F32)
    slot_first = first.astype(F32) * cap + jnp.sum(
        jnp.where(names_first, earlier, 0.0), axis=0, keepdims=True
    )
    slot_second = second.astype(F32) * cap + jnp.sum(
        jnp.where(names_second, earlier, 0.0), axis=0, keepdims=True
    )
    meta_row = lax.broadcasted_iota(jnp.int32, (8, tokens), 0)
    meta[z, :, 0:tokens] = jnp.where(
        meta_row == 0,
        slot_first,
        jnp.where(
            meta_row == 1, slot_second, jnp.where(meta_row == 2, gates[0:1, :], gates[1:2, :])
        ),
    )
    meta[z, :, tokens : 2 * tokens] = jnp.zeros((8, tokens), F32)

    pl.semaphore_wait(barrier, PLANES - 1 + EXPERTS - 1 + 2)

    def gate_up_copy(c):
        return remote(
            w_gate_up.at[pl.ds(pl.multiple_of(c * span, span), span)],
            gate_up_w.at[1, pl.ds(pl.multiple_of(c * span, span), span)],
            gu_send.at[c],
            gu_recv.at[c],
            partner,
        )

    def down_copy(c):
        return remote(
            w_down.at[:, cols(c)],
            down_w.at[c, pl.ds(inner, inner)],
            wd_send.at[c],
            wd_recv.at[c],
            partner,
        )

    def meta_copy(to, plane):
        return remote(
            meta.at[plane], meta.at[plane], meta_send.at[to], meta_recv.at[plane], along_z(to)
        )

    def up_copy(c, plane):
        at = c * PLANES + plane
        return remote(raw.at[c, plane], raw.at[c, plane], up_send.at[at], raw_recv.at[at], me + 1)

    def dn_copy(c, plane):
        at = c * PLANES + plane
        return remote(raw.at[c, plane], raw.at[c, plane], dn_send.at[at], raw_recv.at[at], me - 1)

    def pass_on(c, plane, act_on):
        @pl.when((plane <= z) & (z < PLANES - 1))
        def _():
            act_on(up_copy(c, plane))

        @pl.when((plane >= z) & (z > 0))
        def _():
            act_on(dn_copy(c, plane))

    def go_copy(c, plane, e, to):
        at = c * PLANES + plane
        return remote(
            sorted_rows.at[c, plane, e],
            rows.at[c, plane, rank],
            go_send.at[at],
            go_recv.at[at],
            to,
        )

    def go_all(c, plane):
        at = c * PLANES + plane
        blocks = pl.ds(0, EXPERTS - 1)
        return remote(
            sorted_rows.at[c, plane, blocks],
            rows.at[c, plane, blocks],
            go_send.at[at],
            go_recv.at[at],
            me,
        )

    slot_row = lax.broadcasted_iota(jnp.int32, (slots, tokens), 0).astype(F32)

    def sort_and_send(c, plane):
        placed = (
            jnp.where(slot_row == meta[plane, 0:1, 0:tokens], 1.0, 0.0)
            + jnp.where(slot_row == meta[plane, 1:2, 0:tokens], 1.0, 0.0)
        ).astype(BF16)
        block = jnp.dot(placed, raw[c, plane], preferred_element_type=F32).astype(BF16)
        sorted_rows[c, plane] = block.reshape(EXPERTS, cap, span)
        for e, to in plane_peers:
            go_copy(c, plane, e, to).start()
        rows[c, plane, rank] = sorted_rows[c, plane, rank]

    for i in range(1, PLANES):
        meta_copy(lax.rem(z + i, PLANES), z).start()
    for c in range(PIECES):
        pass_on(c, z, lambda copy: copy.start())
        gate_up_copy(c).start()

    def own_dispatch(c, carry):
        sort_and_send(c, z)
        return carry

    lax.fori_loop(0, PIECES, own_dispatch, 0)
    for i in range(1, PLANES):
        plane = lax.rem(z + i, PLANES)
        meta_copy(z, plane).wait_recv()

    def dispatch(n, carry):
        c = lax.div(n, PLANES - 1)
        plane = other_plane(lax.rem(n, PLANES - 1) + 1)
        at = c * PLANES + plane
        remote(raw.at[c, plane], raw.at[c, plane], up_send.at[at], raw_recv.at[at], me).wait_recv()
        pass_on(c, plane, lambda copy: copy.start())
        sort_and_send(c, plane)
        return carry

    lax.fori_loop(0, PIECES * (PLANES - 1), dispatch, 0)
    for c in range(PIECES):
        gate_up_copy(c).wait_send()
    for c in range(DOWN_AHEAD):
        down_copy(c).start()

    own_copies[4].wait()

    def gate_up(c, carry):
        def arrived(plane, carry):
            go_all(c, plane).wait_recv()
            return carry

        lax.fori_loop(0, PLANES, arrived, 0)
        gate_up_copy(c).wait_recv()
        block = rows[c].reshape(PLANES * slots, span)
        for s in range(2):
            w = gate_up_w[s, pl.ds(pl.multiple_of(c * span, span), span), :]
            total_gate_up[s] = total_gate_up[s] + jnp.dot(block, w, preferred_element_type=F32)
        return carry

    total_gate_up[...] = jnp.zeros_like(total_gate_up)
    lax.fori_loop(0, PIECES, gate_up, 0)
    for s in range(2):
        gate = total_gate_up[s, :, 0:inner]
        act[:, s * inner : (s + 1) * inner] = (
            gate / (1.0 + jnp.exp(-gate)) * total_gate_up[s, :, inner : 2 * inner]
        ).astype(BF16)

    def back_copy(c, plane, e, to):
        at = c * PLANES + plane
        return remote(
            piece.at[c, plane, e],
            back.at[c, plane, rank],
            back_send.at[at],
            back_recv.at[at],
            to,
        )

    def back_all(c, plane):
        at = c * PLANES + plane
        blocks = pl.ds(0, EXPERTS - 1)
        return remote(
            piece.at[c, plane, blocks],
            back.at[c, plane, blocks],
            back_send.at[at],
            back_recv.at[at],
            me,
        )

    def down(c):
        own_down(c).wait()
        down_copy(c).wait_recv()

        @pl.when(c + DOWN_AHEAD < BACK_PIECES)
        def _():
            down_copy(c + DOWN_AHEAD).start()

        block = jnp.dot(act[...], down_w[c], preferred_element_type=F32).astype(BF16)
        piece[c] = block.reshape(PLANES, EXPERTS, cap, back_span)

        def send(i, carry):
            plane = jnp.where(i == PLANES, z, other_plane(PLANES - i))
            for e, to in plane_peers:
                back_copy(c, plane, e, to).start()
            back[c, plane, rank] = piece[c, plane, rank]
            return carry

        lax.fori_loop(1, PLANES + 1, send, 0)

    def part_up(c, plane):
        at = c * PLANES + plane
        return remote(
            part.at[c, plane], from_below.at[c, plane], part_send.at[at], below_recv.at[at], me + 1
        )

    def part_down(c, plane):
        at = c * PLANES + plane
        return remote(
            part.at[c, plane], from_above.at[c, plane], part_send.at[at], above_recv.at[at], me - 1
        )

    def combined(c, plane):
        back_all(c, plane).wait_recv()
        weight = jnp.where(
            slot_row == meta[plane, 0:1, 0:tokens], meta[plane, 2:3, 0:tokens], 0.0
        ) + jnp.where(slot_row == meta[plane, 1:2, 0:tokens], meta[plane, 3:4, 0:tokens], 0.0)
        high = weight.astype(BF16)
        low = (weight - high.astype(F32)).astype(BF16)
        both = lax.dot_general(
            jnp.concatenate([high, low], axis=1),
            back[c, plane].reshape(slots, back_span),
            (((0,), (0,)), ((), ())),
            preferred_element_type=F32,
        )
        return both[0:tokens] + both[tokens : 2 * tokens]

    def hand_copy(c):
        return remote(
            layer_out.at[c], out.at[:, cols(c)], hand_send.at[c], hand_recv.at[c], me, after
        )

    def combine(c):
        def send(i, carry):
            plane = other_plane(PLANES - i)
            total_part[...] = combined(c, plane)

            @pl.when((plane > z) & (z > 0))
            def _():
                part_up(c, plane).wait_recv()
                total_part[...] += from_below[c, plane].astype(F32)

            @pl.when((plane < z) & (z < PLANES - 1))
            def _():
                part_down(c, plane).wait_recv()
                total_part[...] += from_above[c, plane].astype(F32)

            part[c, plane] = total_part[...].astype(BF16)

            @pl.when(plane > z)
            def _():
                part_up(c, plane).start()

            @pl.when(plane < z)
            def _():
                part_down(c, plane).start()

            return carry

        lax.fori_loop(1, PLANES, send, 0)
        home[c] = hidden[:, cols(c)].astype(F32) + combined(c, z)

    def finish(c):
        @pl.when(z > 0)
        def _():
            part_up(c, z).wait_recv()
            home[c] += from_below[c, z].astype(F32)

        @pl.when(z < PLANES - 1)
        def _():
            part_down(c, z).wait_recv()
            home[c] += from_above[c, z].astype(F32)

        layer_out[c] = home[c].astype(BF16)
        hand_copy(c).start()

    def dispatch_left(c, carry):
        def sent_plane(plane, carry):
            go_all(c, plane).wait_send()
            pass_on(c, plane, lambda copy: copy.wait_send())
            return carry

        lax.fori_loop(0, PLANES, sent_plane, 0)
        return carry

    def back_left(c):
        down_copy(c).wait_send()

        def sent_plane(plane, carry):
            back_all(c, plane).wait_send()
            return carry

        lax.fori_loop(0, PLANES, sent_plane, 0)
        for i in range(1, PLANES):
            part_up(c, lax.rem(z + i, PLANES)).wait_send()

    def way_back(c, carry):
        @pl.when(c + AHEAD < BACK_PIECES)
        def _():
            down(c + AHEAD)

        combine(c)

        @pl.when(c > 0)
        def _():
            finish(c - 1)
            back_left(c - 1)

        return carry

    for c in range(AHEAD):
        down(c)
    lax.fori_loop(0, PIECES, dispatch_left, 0)
    for i in range(1, PLANES):
        meta_copy(lax.rem(z + i, PLANES), z).wait_send()
    lax.fori_loop(0, BACK_PIECES, way_back, 0)
    finish(BACK_PIECES - 1)
    back_left(BACK_PIECES - 1)

    for c in range(BACK_PIECES):
        hand_copy(c).wait()


def local(hidden_rows, norm_gain, routes, gates, w_gate_up, w_down):
    hidden = hidden_rows[0]
    tokens, width = hidden.shape
    picks = routes.shape[2]
    cap = tokens * picks // EXPERTS
    inner = w_down.shape[2]
    span = width // PIECES
    back_span = width // BACK_PIECES
    slots = EXPERTS * cap
    hbm = pl.BlockSpec(memory_space=pltpu.HBM)
    dma = pltpu.SemaphoreType.DMA
    blocks = pltpu.VMEM((PIECES, PLANES, EXPERTS, cap, span), BF16)
    per_plane = pltpu.VMEM((PIECES, PLANES, tokens, span), BF16)
    back_blocks = pltpu.VMEM((BACK_PIECES, PLANES, EXPERTS, cap, back_span), BF16)
    back_per_plane = pltpu.VMEM((BACK_PIECES, PLANES, tokens, back_span), BF16)
    handoff = pl.pallas_call(
        layer_kernel,
        out_shape=jax.ShapeDtypeStruct((tokens, width), BF16),
        in_specs=[hbm] * 6,
        out_specs=hbm,
        scratch_shapes=[
            pltpu.VMEM((tokens, width), BF16),
            pltpu.VMEM((1, width), F32),
            pltpu.VMEM((picks, tokens), jnp.int32),
            pltpu.VMEM((picks, tokens), F32),
            per_plane,
            pltpu.VMEM((PLANES, 8, 2 * tokens), F32),
            blocks,
            blocks,
            pltpu.VMEM((2, width, 2 * inner), BF16),
            pltpu.VMEM((BACK_PIECES, 2 * inner, back_span), BF16),
            pltpu.VMEM((2, PLANES * slots, 2 * inner), F32),
            pltpu.VMEM((PLANES * slots, 2 * inner), BF16),
            back_blocks,
            back_blocks,
            back_per_plane,
            back_per_plane,
            back_per_plane,
            pltpu.VMEM((tokens, back_span), F32),
            pltpu.VMEM((BACK_PIECES, tokens, back_span), F32),
            pltpu.VMEM((BACK_PIECES, tokens, back_span), BF16),
            dma((5 + BACK_PIECES,)),
            dma((PIECES,)),
            dma((PIECES,)),
            dma((BACK_PIECES,)),
            dma((BACK_PIECES,)),
            dma((PIECES * PLANES,)),
            dma((PIECES * PLANES,)),
            dma((PIECES * PLANES,)),
            dma((PLANES,)),
            dma((PLANES,)),
            dma((PIECES * PLANES,)),
            dma((PIECES * PLANES,)),
            dma((BACK_PIECES * PLANES,)),
            dma((BACK_PIECES * PLANES,)),
            dma((BACK_PIECES * PLANES,)),
            dma((BACK_PIECES * PLANES,)),
            dma((BACK_PIECES * PLANES,)),
            dma((BACK_PIECES,)),
            dma((BACK_PIECES,)),
        ],
        compiler_params=pltpu.CompilerParams(
            collective_id=0, has_side_effects=True, vmem_limit_bytes=62 * 1024 * 1024
        ),
        cost_estimate=pl.CostEstimate(
            flops=6 * EXPERTS * SHARDS * cap * width * inner,
            bytes_accessed=2 * (tokens * width * 2 + 3 * width * inner),
            transcendentals=EXPERTS * SHARDS * cap * inner,
        ),
    )(hidden, norm_gain, routes[0].T, gates[0].T, w_gate_up[0, 0], w_down[0, 0])
    return handoff[None]


def solution(mesh):
    in_specs = (
        P("section", "expert", None),
        P("section", None),
        P("section", "expert", None),
        P("section", "expert", None),
        P("section", "expert", None, None),
        P("section", "expert", None, None),
    )
    out_specs = P("section", "expert", None)
    return jax.shard_map(local, mesh=mesh, in_specs=in_specs, out_specs=out_specs, check_vma=False)
```

```python
import jax
import jax.numpy as jnp
from jax import lax
from jax.experimental import pallas as pl
from jax.experimental.pallas import tpu as pltpu
from jax.sharding import PartitionSpec as P

EXPERTS = 8
SHARDS = 8
PLANES = 4
SECTIONS = 8
PIECES = 4
BACK_PIECES = 7
AHEAD = 2
DOWN_AHEAD = 3
HOP_STEPS = 1
MESH = pl.DeviceIdType.MESH
BF16 = jnp.bfloat16
F32 = jnp.float32


def layer_kernel(
    hidden_hbm,
    gain_hbm,
    routes_hbm,
    gates_hbm,
    w_gate_up,
    w_down,
    out,
    hidden,
    gain,
    routes,
    gates,
    raw,
    meta,
    sorted_rows,
    rows,
    gate_up_w,
    down_w,
    total_gate_up,
    act,
    piece,
    back,
    part,
    from_below,
    from_above,
    total_part,
    home,
    layer_out,
    in_sem,
    gu_send,
    gu_recv,
    wd_send,
    wd_recv,
    up_send,
    dn_send,
    raw_recv,
    meta_send,
    meta_recv,
    go_send,
    go_recv,
    back_send,
    back_recv,
    part_send,
    below_recv,
    above_recv,
    hand_send,
    hand_recv,
):
    tokens, width = hidden.shape
    cap = rows.shape[3]
    inner = w_down.shape[0]
    slots = EXPERTS * cap
    span = width // PIECES
    back_span = width // BACK_PIECES

    section = lax.axis_index("section")
    me = lax.axis_index("expert")
    z = lax.rem(me, PLANES)
    column = lax.div(me, PLANES)
    y = lax.rem(column, 4)
    rank = lax.div(me, SHARDS)
    y_half, y_odd = lax.div(y, 2), lax.rem(y, 2)
    side = lax.rem(y_half + y_odd, 2)
    partner = (column - y_odd + 1 - y_odd) * PLANES + z
    after = lax.rem(section + 1, SECTIONS)
    before = lax.rem(section + SECTIONS - 1, SECTIONS)
    flip = lax.div(z, 2)
    z_low = z + flip * (PLANES - 1 - 2 * z)

    def in_plane(e):
        half = lax.rem(e, 2)
        return (lax.div(e, 2) * 4 + 2 * half + lax.rem(half + side, 2)) * PLANES + z

    def along_z(plane):
        return column * PLANES + plane

    def other_plane(i):
        low = jnp.where(i - 1 < z_low, i - 1, i)
        return low + flip * (PLANES - 1 - 2 * low)

    def cols(c):
        return pl.ds(pl.multiple_of(c * back_span, back_span), back_span)

    def remote(src, dst, send, recv, to, to_section=None):
        return pltpu.make_async_remote_copy(
            src_ref=src,
            dst_ref=dst,
            send_sem=send,
            recv_sem=recv,
            device_id=(section if to_section is None else to_section, to),
            device_id_type=MESH,
        )

    others = [lax.rem(rank + d, EXPERTS) for d in range(1, EXPERTS)]
    plane_peers = [(e, in_plane(e)) for e in others]

    barrier = pltpu.get_barrier_semaphore()

    def greet(to, to_section):
        pl.semaphore_signal(barrier, inc=1, device_id=(to_section, to), device_id_type=MESH)

    for i in range(1, PLANES):
        greet(along_z(lax.rem(z + i, PLANES)), section)
    for _, to in plane_peers:
        greet(to, section)
    greet(partner, section)
    greet(me, before)

    own_copies = [
        pltpu.make_async_copy(hidden_hbm, hidden, in_sem.at[0]),
        pltpu.make_async_copy(gain_hbm, gain, in_sem.at[1]),
        pltpu.make_async_copy(routes_hbm, routes, in_sem.at[2]),
        pltpu.make_async_copy(gates_hbm, gates, in_sem.at[3]),
        pltpu.make_async_copy(w_gate_up, gate_up_w.at[0], in_sem.at[4]),
    ]
    for copy in own_copies:
        copy.start()

    def own_down(c):
        return pltpu.make_async_copy(
            w_down.at[:, cols(c)], down_w.at[c, pl.ds(0, inner)], in_sem.at[5 + c]
        )

    for c in range(BACK_PIECES):
        own_down(c).start()
    for copy in own_copies[:4]:
        copy.wait()

    rows_f32 = hidden[...].astype(F32)
    scale = lax.rsqrt(jnp.mean(rows_f32 * rows_f32, axis=1, keepdims=True) + 1e-06)
    for c in range(PIECES):
        lo, hi = c * span, (c + 1) * span
        raw[c, z] = (hidden[:, lo:hi].astype(F32) * scale * gain[:, lo:hi]).astype(BF16)

    names = lax.broadcasted_iota(jnp.int32, (16, tokens), 0)
    first, second = routes[0:1, :], routes[1:2, :]
    names_first, names_second = names == first, names == second
    one_hot = (jnp.where(names_first, 1.0, 0.0) + jnp.where(names_second, 1.0, 0.0)).astype(BF16)
    above = jnp.where(
        lax.broadcasted_iota(jnp.int32, (tokens, tokens), 0)
        < lax.broadcasted_iota(jnp.int32, (tokens, tokens), 1),
        1.0,
        0.0,
    ).astype(BF16)
    earlier = jnp.dot(one_hot, above, preferred_element_type=F32)
    slot_first = first.astype(F32) * cap + jnp.sum(
        jnp.where(names_first, earlier, 0.0), axis=0, keepdims=True
    )
    slot_second = second.astype(F32) * cap + jnp.sum(
        jnp.where(names_second, earlier, 0.0), axis=0, keepdims=True
    )
    meta_row = lax.broadcasted_iota(jnp.int32, (8, tokens), 0)
    meta[z, :, 0:tokens] = jnp.where(
        meta_row == 0,
        slot_first,
        jnp.where(
            meta_row == 1, slot_second, jnp.where(meta_row == 2, gates[0:1, :], gates[1:2, :])
        ),
    )
    meta[z, :, tokens : 2 * tokens] = jnp.zeros((8, tokens), F32)

    pl.semaphore_wait(barrier, PLANES - 1 + EXPERTS - 1 + 2)

    def gate_up_copy(c):
        return remote(
            w_gate_up.at[pl.ds(pl.multiple_of(c * span, span), span)],
            gate_up_w.at[1, pl.ds(pl.multiple_of(c * span, span), span)],
            gu_send.at[c],
            gu_recv.at[c],
            partner,
        )

    def down_copy(c):
        return remote(
            w_down.at[:, cols(c)],
            down_w.at[c, pl.ds(inner, inner)],
            wd_send.at[c],
            wd_recv.at[c],
            partner,
        )

    def meta_copy(to, plane):
        return remote(
            meta.at[plane], meta.at[plane], meta_send.at[to], meta_recv.at[plane], along_z(to)
        )

    def up_copy(c, plane):
        at = c * PLANES + plane
        return remote(raw.at[c, plane], raw.at[c, plane], up_send.at[at], raw_recv.at[at], me + 1)

    def dn_copy(c, plane):
        at = c * PLANES + plane
        return remote(raw.at[c, plane], raw.at[c, plane], dn_send.at[at], raw_recv.at[at], me - 1)

    def pass_on(c, plane, act_on):
        @pl.when((plane <= z) & (z < PLANES - 1))
        def _():
            act_on(up_copy(c, plane))

        @pl.when((plane >= z) & (z > 0))
        def _():
            act_on(dn_copy(c, plane))

    def go_copy(c, plane, e, to):
        at = c * PLANES + plane
        return remote(
            sorted_rows.at[c, plane, e],
            rows.at[c, plane, rank],
            go_send.at[at],
            go_recv.at[at],
            to,
        )

    def go_all(c, plane):
        at = c * PLANES + plane
        blocks = pl.ds(0, EXPERTS - 1)
        return remote(
            sorted_rows.at[c, plane, blocks],
            rows.at[c, plane, blocks],
            go_send.at[at],
            go_recv.at[at],
            me,
        )

    slot_row = lax.broadcasted_iota(jnp.int32, (slots, tokens), 0).astype(F32)

    def sort_and_send(c, plane):
        placed = (
            jnp.where(slot_row == meta[plane, 0:1, 0:tokens], 1.0, 0.0)
            + jnp.where(slot_row == meta[plane, 1:2, 0:tokens], 1.0, 0.0)
        ).astype(BF16)
        block = jnp.dot(placed, raw[c, plane], preferred_element_type=F32).astype(BF16)
        sorted_rows[c, plane] = block.reshape(EXPERTS, cap, span)
        for e, to in plane_peers:
            go_copy(c, plane, e, to).start()
        rows[c, plane, rank] = sorted_rows[c, plane, rank]

    for i in range(1, PLANES):
        meta_copy(lax.rem(z + i, PLANES), z).start()
    for c in range(PIECES):
        pass_on(c, z, lambda copy: copy.start())
        gate_up_copy(c).start()

    def own_dispatch(c, carry):
        sort_and_send(c, z)
        return carry

    lax.fori_loop(0, PIECES, own_dispatch, 0)
    for i in range(1, PLANES):
        plane = lax.rem(z + i, PLANES)
        meta_copy(z, plane).wait_recv()

    def dispatch(n, carry):
        c = lax.div(n, PLANES - 1)
        plane = other_plane(lax.rem(n, PLANES - 1) + 1)
        at = c * PLANES + plane
        remote(raw.at[c, plane], raw.at[c, plane], up_send.at[at], raw_recv.at[at], me).wait_recv()
        pass_on(c, plane, lambda copy: copy.start())
        sort_and_send(c, plane)
        return carry

    lax.fori_loop(0, PIECES * (PLANES - 1), dispatch, 0)
    for c in range(PIECES):
        gate_up_copy(c).wait_send()
    for c in range(DOWN_AHEAD):
        down_copy(c).start()

    own_copies[4].wait()

    def gate_up(c, carry):
        def arrived(plane, carry):
            go_all(c, plane).wait_recv()
            return carry

        lax.fori_loop(0, PLANES, arrived, 0)
        gate_up_copy(c).wait_recv()
        block = rows[c].reshape(PLANES * slots, span)
        for s in range(2):
            w = gate_up_w[s, pl.ds(pl.multiple_of(c * span, span), span), :]
            total_gate_up[s] = total_gate_up[s] + jnp.dot(block, w, preferred_element_type=F32)
        return carry

    total_gate_up[...] = jnp.zeros_like(total_gate_up)
    lax.fori_loop(0, PIECES, gate_up, 0)
    for s in range(2):
        gate = total_gate_up[s, :, 0:inner]
        act[:, s * inner : (s + 1) * inner] = (
            gate / (1.0 + jnp.exp(-gate)) * total_gate_up[s, :, inner : 2 * inner]
        ).astype(BF16)

    def back_copy(c, plane, e, to):
        at = c * PLANES + plane
        return remote(
            piece.at[c, plane, e],
            back.at[c, plane, rank],
            back_send.at[at],
            back_recv.at[at],
            to,
        )

    def back_all(c, plane):
        at = c * PLANES + plane
        blocks = pl.ds(0, EXPERTS - 1)
        return remote(
            piece.at[c, plane, blocks],
            back.at[c, plane, blocks],
            back_send.at[at],
            back_recv.at[at],
            me,
        )

    def down(c):
        own_down(c).wait()
        down_copy(c).wait_recv()

        @pl.when(c + DOWN_AHEAD < BACK_PIECES)
        def _():
            down_copy(c + DOWN_AHEAD).start()

        block = jnp.dot(act[...], down_w[c], preferred_element_type=F32).astype(BF16)
        piece[c] = block.reshape(PLANES, EXPERTS, cap, back_span)

        def send(i, carry):
            plane = jnp.where(i == PLANES, z, other_plane(PLANES - i))
            for e, to in plane_peers:
                back_copy(c, plane, e, to).start()
            back[c, plane, rank] = piece[c, plane, rank]
            return carry

        lax.fori_loop(1, PLANES + 1, send, 0)

    def part_up(c, plane):
        at = c * PLANES + plane
        return remote(
            part.at[c, plane], from_below.at[c, plane], part_send.at[at], below_recv.at[at], me + 1
        )

    def part_down(c, plane):
        at = c * PLANES + plane
        return remote(
            part.at[c, plane], from_above.at[c, plane], part_send.at[at], above_recv.at[at], me - 1
        )

    def combined(c, plane):
        back_all(c, plane).wait_recv()
        weight = jnp.where(
            slot_row == meta[plane, 0:1, 0:tokens], meta[plane, 2:3, 0:tokens], 0.0
        ) + jnp.where(slot_row == meta[plane, 1:2, 0:tokens], meta[plane, 3:4, 0:tokens], 0.0)
        high = weight.astype(BF16)
        low = (weight - high.astype(F32)).astype(BF16)
        both = lax.dot_general(
            jnp.concatenate([high, low], axis=1),
            back[c, plane].reshape(slots, back_span),
            (((0,), (0,)), ((), ())),
            preferred_element_type=F32,
        )
        return both[0:tokens] + both[tokens : 2 * tokens]

    def hand_copy(c):
        return remote(
            layer_out.at[c], out.at[:, cols(c)], hand_send.at[c], hand_recv.at[c], me, after
        )

    def combine(c):
        def one(i, carry):
            plane = other_plane(PLANES - i)
            total_part[c, plane] = combined(c, plane)

            @pl.when((plane > z) & (z == 0))
            def _():
                part[c, plane] = total_part[c, plane].astype(BF16)
                part_up(c, plane).start()

            @pl.when((plane < z) & (z == PLANES - 1))
            def _():
                part[c, plane] = total_part[c, plane].astype(BF16)
                part_down(c, plane).start()

            return carry

        lax.fori_loop(1, PLANES, one, 0)
        home[c] = hidden[:, cols(c)].astype(F32) + combined(c, z)

    def add_up(c):
        def one(i, carry):
            plane = other_plane(PLANES - i)

            @pl.when(plane > z)
            def _():
                part_up(c, plane).wait_recv()
                part[c, plane] = (
                    total_part[c, plane] + from_below[c, plane].astype(F32)
                ).astype(BF16)
                part_up(c, plane).start()

            return carry

        lax.fori_loop(1, PLANES, one, 0)

    def add_down(c):
        def one(i, carry):
            plane = other_plane(PLANES - i)

            @pl.when(plane < z)
            def _():
                part_down(c, plane).wait_recv()
                part[c, plane] = (
                    total_part[c, plane] + from_above[c, plane].astype(F32)
                ).astype(BF16)
                part_down(c, plane).start()

            return carry

        lax.fori_loop(1, PLANES, one, 0)

    def finish(c):
        @pl.when(z > 0)
        def _():
            part_up(c, z).wait_recv()
            home[c] += from_below[c, z].astype(F32)

        @pl.when(z < PLANES - 1)
        def _():
            part_down(c, z).wait_recv()
            home[c] += from_above[c, z].astype(F32)

        layer_out[c] = home[c].astype(BF16)
        hand_copy(c).start()

    def dispatch_left(c, carry):
        def sent_plane(plane, carry):
            go_all(c, plane).wait_send()
            pass_on(c, plane, lambda copy: copy.wait_send())
            return carry

        lax.fori_loop(0, PLANES, sent_plane, 0)
        return carry

    def back_left(c):
        down_copy(c).wait_send()

        def sent_plane(plane, carry):
            back_all(c, plane).wait_send()
            return carry

        lax.fori_loop(0, PLANES, sent_plane, 0)
        for i in range(1, PLANES):
            part_up(c, lax.rem(z + i, PLANES)).wait_send()

    hops_up, hops_down = z * HOP_STEPS, (PLANES - 1 - z) * HOP_STEPS
    hops_home = (PLANES - 1 - z_low) * HOP_STEPS

    def way_back(n, carry):
        @pl.when(n + AHEAD < BACK_PIECES)
        def _():
            down(n + AHEAD)

        @pl.when(n < BACK_PIECES)
        def _():
            combine(n)

        @pl.when((z > 0) & (z < PLANES - 1) & (n >= hops_up) & (n - hops_up < BACK_PIECES))
        def _():
            add_up(n - hops_up)

        @pl.when((z > 0) & (z < PLANES - 1) & (n >= hops_down) & (n - hops_down < BACK_PIECES))
        def _():
            add_down(n - hops_down)

        @pl.when((n >= hops_home) & (n - hops_home < BACK_PIECES))
        def _():
            finish(n - hops_home)

        @pl.when((n > hops_home) & (n - hops_home <= BACK_PIECES))
        def _():
            back_left(n - hops_home - 1)

        return carry

    for c in range(AHEAD):
        down(c)
    lax.fori_loop(0, PIECES, dispatch_left, 0)
    for i in range(1, PLANES):
        meta_copy(lax.rem(z + i, PLANES), z).wait_send()
    lax.fori_loop(0, BACK_PIECES + (PLANES - 1) * HOP_STEPS + 1, way_back, 0)

    for c in range(BACK_PIECES):
        hand_copy(c).wait()


def local(hidden_rows, norm_gain, routes, gates, w_gate_up, w_down):
    hidden = hidden_rows[0]
    tokens, width = hidden.shape
    picks = routes.shape[2]
    cap = tokens * picks // EXPERTS
    inner = w_down.shape[2]
    span = width // PIECES
    back_span = width // BACK_PIECES
    slots = EXPERTS * cap
    hbm = pl.BlockSpec(memory_space=pltpu.HBM)
    dma = pltpu.SemaphoreType.DMA
    blocks = pltpu.VMEM((PIECES, PLANES, EXPERTS, cap, span), BF16)
    per_plane = pltpu.VMEM((PIECES, PLANES, tokens, span), BF16)
    back_blocks = pltpu.VMEM((BACK_PIECES, PLANES, EXPERTS, cap, back_span), BF16)
    back_per_plane = pltpu.VMEM((BACK_PIECES, PLANES, tokens, back_span), BF16)
    handoff = pl.pallas_call(
        layer_kernel,
        out_shape=jax.ShapeDtypeStruct((tokens, width), BF16),
        in_specs=[hbm] * 6,
        out_specs=hbm,
        scratch_shapes=[
            pltpu.VMEM((tokens, width), BF16),
            pltpu.VMEM((1, width), F32),
            pltpu.VMEM((picks, tokens), jnp.int32),
            pltpu.VMEM((picks, tokens), F32),
            per_plane,
            pltpu.VMEM((PLANES, 8, 2 * tokens), F32),
            blocks,
            blocks,
            pltpu.VMEM((2, width, 2 * inner), BF16),
            pltpu.VMEM((BACK_PIECES, 2 * inner, back_span), BF16),
            pltpu.VMEM((2, PLANES * slots, 2 * inner), F32),
            pltpu.VMEM((PLANES * slots, 2 * inner), BF16),
            back_blocks,
            back_blocks,
            back_per_plane,
            back_per_plane,
            back_per_plane,
            pltpu.VMEM((BACK_PIECES, PLANES, tokens, back_span), F32),
            pltpu.VMEM((BACK_PIECES, tokens, back_span), F32),
            pltpu.VMEM((BACK_PIECES, tokens, back_span), BF16),
            dma((5 + BACK_PIECES,)),
            dma((PIECES,)),
            dma((PIECES,)),
            dma((BACK_PIECES,)),
            dma((BACK_PIECES,)),
            dma((PIECES * PLANES,)),
            dma((PIECES * PLANES,)),
            dma((PIECES * PLANES,)),
            dma((PLANES,)),
            dma((PLANES,)),
            dma((PIECES * PLANES,)),
            dma((PIECES * PLANES,)),
            dma((BACK_PIECES * PLANES,)),
            dma((BACK_PIECES * PLANES,)),
            dma((BACK_PIECES * PLANES,)),
            dma((BACK_PIECES * PLANES,)),
            dma((BACK_PIECES * PLANES,)),
            dma((BACK_PIECES,)),
            dma((BACK_PIECES,)),
        ],
        compiler_params=pltpu.CompilerParams(
            collective_id=0, has_side_effects=True, vmem_limit_bytes=62 * 1024 * 1024
        ),
        cost_estimate=pl.CostEstimate(
            flops=6 * EXPERTS * SHARDS * cap * width * inner,
            bytes_accessed=2 * (tokens * width * 2 + 3 * width * inner),
            transcendentals=EXPERTS * SHARDS * cap * inner,
        ),
    )(hidden, norm_gain, routes[0].T, gates[0].T, w_gate_up[0, 0], w_down[0, 0])
    return handoff[None]


def solution(mesh):
    in_specs = (
        P("section", "expert", None),
        P("section", None),
        P("section", "expert", None),
        P("section", "expert", None),
        P("section", "expert", None, None),
        P("section", "expert", None, None),
    )
    out_specs = P("section", "expert", None)
    return jax.shard_map(local, mesh=mesh, in_specs=in_specs, out_specs=out_specs, check_vma=False)
```

```python
import jax
import jax.numpy as jnp
from jax import lax
from jax.experimental import pallas as pl
from jax.experimental.pallas import tpu as pltpu
from jax.sharding import PartitionSpec as P

EXPERTS = 8
SHARDS = 8
PLANES = 4
SECTIONS = 8
PIECES = 4
BACK_PIECES = 7
AHEAD = 2
DOWN_AHEAD = 3
MESH = pl.DeviceIdType.MESH
BF16 = jnp.bfloat16
F32 = jnp.float32


def layer_kernel(
    hidden_hbm,
    gain_hbm,
    routes_hbm,
    gates_hbm,
    w_gate_up,
    w_down,
    out,
    hidden,
    gain,
    routes,
    gates,
    raw,
    meta,
    sorted_rows,
    rows,
    gate_up_w,
    down_w,
    total_gate_up,
    act,
    piece,
    back,
    part,
    from_below,
    from_above,
    total_part,
    home,
    layer_out,
    gate_matrix,
    in_sem,
    gu_send,
    gu_recv,
    wd_send,
    wd_recv,
    up_send,
    dn_send,
    raw_recv,
    meta_send,
    meta_recv,
    go_send,
    go_recv,
    back_send,
    back_recv,
    part_send,
    below_recv,
    above_recv,
    hand_send,
    hand_recv,
):
    tokens, width = hidden.shape
    cap = rows.shape[3]
    inner = w_down.shape[0]
    slots = EXPERTS * cap
    span = width // PIECES
    back_span = width // BACK_PIECES

    section = lax.axis_index("section")
    me = lax.axis_index("expert")
    z = lax.rem(me, PLANES)
    column = lax.div(me, PLANES)
    y = lax.rem(column, 4)
    rank = lax.div(me, SHARDS)
    y_half, y_odd = lax.div(y, 2), lax.rem(y, 2)
    side = lax.rem(y_half + y_odd, 2)
    partner = (column - y_odd + 1 - y_odd) * PLANES + z
    after = lax.rem(section + 1, SECTIONS)
    before = lax.rem(section + SECTIONS - 1, SECTIONS)
    flip = lax.div(z, 2)
    z_low = z + flip * (PLANES - 1 - 2 * z)

    def in_plane(e):
        half = lax.rem(e, 2)
        return (lax.div(e, 2) * 4 + 2 * half + lax.rem(half + side, 2)) * PLANES + z

    def along_z(plane):
        return column * PLANES + plane

    def other_plane(i):
        low = jnp.where(i - 1 < z_low, i - 1, i)
        return low + flip * (PLANES - 1 - 2 * low)

    def cols(c):
        return pl.ds(pl.multiple_of(c * back_span, back_span), back_span)

    def remote(src, dst, send, recv, to, to_section=None):
        return pltpu.make_async_remote_copy(
            src_ref=src,
            dst_ref=dst,
            send_sem=send,
            recv_sem=recv,
            device_id=(section if to_section is None else to_section, to),
            device_id_type=MESH,
        )

    others = [lax.rem(rank + d, EXPERTS) for d in range(1, EXPERTS)]
    plane_peers = [(e, in_plane(e)) for e in others]

    barrier = pltpu.get_barrier_semaphore()

    def greet(to, to_section):
        pl.semaphore_signal(barrier, inc=1, device_id=(to_section, to), device_id_type=MESH)

    for i in range(1, PLANES):
        greet(along_z(lax.rem(z + i, PLANES)), section)
    for _, to in plane_peers:
        greet(to, section)
    greet(partner, section)
    greet(me, before)

    own_copies = [
        pltpu.make_async_copy(hidden_hbm, hidden, in_sem.at[0]),
        pltpu.make_async_copy(gain_hbm, gain, in_sem.at[1]),
        pltpu.make_async_copy(routes_hbm, routes, in_sem.at[2]),
        pltpu.make_async_copy(gates_hbm, gates, in_sem.at[3]),
        pltpu.make_async_copy(w_gate_up, gate_up_w.at[0], in_sem.at[4]),
    ]
    for copy in own_copies:
        copy.start()

    def own_down(c):
        return pltpu.make_async_copy(
            w_down.at[:, cols(c)], down_w.at[c, pl.ds(0, inner)], in_sem.at[5 + c]
        )

    for c in range(BACK_PIECES):
        own_down(c).start()
    for copy in own_copies[:4]:
        copy.wait()

    rows_f32 = hidden[...].astype(F32)
    scale = lax.rsqrt(jnp.mean(rows_f32 * rows_f32, axis=1, keepdims=True) + 1e-06)
    for c in range(PIECES):
        lo, hi = c * span, (c + 1) * span
        raw[c, z] = (hidden[:, lo:hi].astype(F32) * scale * gain[:, lo:hi]).astype(BF16)

    names = lax.broadcasted_iota(jnp.int32, (16, tokens), 0)
    first, second = routes[0:1, :], routes[1:2, :]
    names_first, names_second = names == first, names == second
    one_hot = (jnp.where(names_first, 1.0, 0.0) + jnp.where(names_second, 1.0, 0.0)).astype(BF16)
    above = jnp.where(
        lax.broadcasted_iota(jnp.int32, (tokens, tokens), 0)
        < lax.broadcasted_iota(jnp.int32, (tokens, tokens), 1),
        1.0,
        0.0,
    ).astype(BF16)
    earlier = jnp.dot(one_hot, above, preferred_element_type=F32)
    slot_first = first.astype(F32) * cap + jnp.sum(
        jnp.where(names_first, earlier, 0.0), axis=0, keepdims=True
    )
    slot_second = second.astype(F32) * cap + jnp.sum(
        jnp.where(names_second, earlier, 0.0), axis=0, keepdims=True
    )
    meta_row = lax.broadcasted_iota(jnp.int32, (8, tokens), 0)
    meta[z, :, 0:tokens] = jnp.where(
        meta_row == 0,
        slot_first,
        jnp.where(
            meta_row == 1, slot_second, jnp.where(meta_row == 2, gates[0:1, :], gates[1:2, :])
        ),
    )
    meta[z, :, tokens : 2 * tokens] = jnp.zeros((8, tokens), F32)

    pl.semaphore_wait(barrier, PLANES - 1 + EXPERTS - 1 + 2)

    def gate_up_copy(c):
        return remote(
            w_gate_up.at[pl.ds(pl.multiple_of(c * span, span), span)],
            gate_up_w.at[1, pl.ds(pl.multiple_of(c * span, span), span)],
            gu_send.at[c],
            gu_recv.at[c],
            partner,
        )

    def down_copy(c):
        return remote(
            w_down.at[:, cols(c)],
            down_w.at[c, pl.ds(inner, inner)],
            wd_send.at[c],
            wd_recv.at[c],
            partner,
        )

    def meta_copy(to, plane):
        return remote(
            meta.at[plane], meta.at[plane], meta_send.at[to], meta_recv.at[plane], along_z(to)
        )

    def up_copy(c, plane):
        at = c * PLANES + plane
        return remote(raw.at[c, plane], raw.at[c, plane], up_send.at[at], raw_recv.at[at], me + 1)

    def dn_copy(c, plane):
        at = c * PLANES + plane
        return remote(raw.at[c, plane], raw.at[c, plane], dn_send.at[at], raw_recv.at[at], me - 1)

    def pass_on(c, plane, act_on):
        @pl.when((plane <= z) & (z < PLANES - 1))
        def _():
            act_on(up_copy(c, plane))

        @pl.when((plane >= z) & (z > 0))
        def _():
            act_on(dn_copy(c, plane))

    def go_copy(c, plane, e, to):
        at = c * PLANES + plane
        return remote(
            sorted_rows.at[c, plane, e],
            rows.at[c, plane, rank],
            go_send.at[at],
            go_recv.at[at],
            to,
        )

    def go_all(c, plane):
        at = c * PLANES + plane
        blocks = pl.ds(0, EXPERTS - 1)
        return remote(
            sorted_rows.at[c, plane, blocks],
            rows.at[c, plane, blocks],
            go_send.at[at],
            go_recv.at[at],
            me,
        )

    slot_row = lax.broadcasted_iota(jnp.int32, (slots, tokens), 0).astype(F32)

    def sort_and_send(c, plane):
        placed = (
            jnp.where(slot_row == meta[plane, 0:1, 0:tokens], 1.0, 0.0)
            + jnp.where(slot_row == meta[plane, 1:2, 0:tokens], 1.0, 0.0)
        ).astype(BF16)
        block = jnp.dot(placed, raw[c, plane], preferred_element_type=F32).astype(BF16)
        sorted_rows[c, plane] = block.reshape(EXPERTS, cap, span)
        for e, to in plane_peers:
            go_copy(c, plane, e, to).start()
        rows[c, plane, rank] = sorted_rows[c, plane, rank]

    for i in range(1, PLANES):
        meta_copy(lax.rem(z + i, PLANES), z).start()
    for c in range(PIECES):
        pass_on(c, z, lambda copy: copy.start())
        gate_up_copy(c).start()

    def own_dispatch(c, carry):
        sort_and_send(c, z)
        return carry

    lax.fori_loop(0, PIECES, own_dispatch, 0)
    for i in range(1, PLANES):
        plane = lax.rem(z + i, PLANES)
        meta_copy(z, plane).wait_recv()

    def dispatch(n, carry):
        c = lax.div(n, PLANES - 1)
        plane = other_plane(lax.rem(n, PLANES - 1) + 1)
        at = c * PLANES + plane
        remote(raw.at[c, plane], raw.at[c, plane], up_send.at[at], raw_recv.at[at], me).wait_recv()
        pass_on(c, plane, lambda copy: copy.start())
        sort_and_send(c, plane)
        return carry

    lax.fori_loop(0, PIECES * (PLANES - 1), dispatch, 0)
    for c in range(PIECES):
        gate_up_copy(c).wait_send()
    for c in range(DOWN_AHEAD):
        down_copy(c).start()

    def gate_rows(plane, carry):
        weight = jnp.where(
            slot_row == meta[plane, 0:1, 0:tokens], meta[plane, 2:3, 0:tokens], 0.0
        ) + jnp.where(slot_row == meta[plane, 1:2, 0:tokens], meta[plane, 3:4, 0:tokens], 0.0)
        high = weight.astype(BF16)
        low = (weight - high.astype(F32)).astype(BF16)
        both = jnp.concatenate([high.astype(F32), low.astype(F32)], axis=1)
        gate_matrix[plane] = jnp.transpose(both).astype(BF16)
        return carry

    lax.fori_loop(0, PLANES, gate_rows, 0)
    own_copies[4].wait()

    def gate_up(c, carry):
        def arrived(plane, carry):
            go_all(c, plane).wait_recv()
            return carry

        lax.fori_loop(0, PLANES, arrived, 0)
        gate_up_copy(c).wait_recv()
        block = rows[c].reshape(PLANES * slots, span)
        for s in range(2):
            w = gate_up_w[s, pl.ds(pl.multiple_of(c * span, span), span), :]
            total_gate_up[s] = total_gate_up[s] + jnp.dot(block, w, preferred_element_type=F32)
        return carry

    total_gate_up[...] = jnp.zeros_like(total_gate_up)
    lax.fori_loop(0, PIECES, gate_up, 0)
    for s in range(2):
        gate = total_gate_up[s, :, 0:inner]
        act[:, s * inner : (s + 1) * inner] = (
            gate / (1.0 + jnp.exp(-gate)) * total_gate_up[s, :, inner : 2 * inner]
        ).astype(BF16)

    def back_copy(c, plane, e, to):
        at = c * PLANES + plane
        return remote(
            piece.at[c, plane, e],
            back.at[c, plane, rank],
            back_send.at[at],
            back_recv.at[at],
            to,
        )

    def back_all(c, plane):
        at = c * PLANES + plane
        blocks = pl.ds(0, EXPERTS - 1)
        return remote(
            piece.at[c, plane, blocks],
            back.at[c, plane, blocks],
            back_send.at[at],
            back_recv.at[at],
            me,
        )

    def down(c):
        own_down(c).wait()
        down_copy(c).wait_recv()

        @pl.when(c + DOWN_AHEAD < BACK_PIECES)
        def _():
            down_copy(c + DOWN_AHEAD).start()

        block = jnp.dot(act[...], down_w[c], preferred_element_type=F32).astype(BF16)
        piece[c] = block.reshape(PLANES, EXPERTS, cap, back_span)

        def send(i, carry):
            plane = jnp.where(i == PLANES, z, other_plane(PLANES - i))
            for e, to in plane_peers:
                back_copy(c, plane, e, to).start()
            back[c, plane, rank] = piece[c, plane, rank]
            return carry

        lax.fori_loop(1, PLANES + 1, send, 0)

    def part_up(c, plane):
        at = c * PLANES + plane
        return remote(
            part.at[c, plane], from_below.at[c, plane], part_send.at[at], below_recv.at[at], me + 1
        )

    def part_down(c, plane):
        at = c * PLANES + plane
        return remote(
            part.at[c, plane], from_above.at[c, plane], part_send.at[at], above_recv.at[at], me - 1
        )

    def combined(c, plane):
        back_all(c, plane).wait_recv()
        both = jnp.dot(
            gate_matrix[plane],
            back[c, plane].reshape(slots, back_span),
            preferred_element_type=F32,
        )
        return both[0:tokens] + both[tokens : 2 * tokens]

    def hand_copy(c):
        return remote(
            layer_out.at[c], out.at[:, cols(c)], hand_send.at[c], hand_recv.at[c], me, after
        )

    def combine(c):
        def send(i, carry):
            plane = other_plane(PLANES - i)
            total_part[...] = combined(c, plane)

            @pl.when((plane > z) & (z > 0))
            def _():
                part_up(c, plane).wait_recv()
                total_part[...] += from_below[c, plane].astype(F32)

            @pl.when((plane < z) & (z < PLANES - 1))
            def _():
                part_down(c, plane).wait_recv()
                total_part[...] += from_above[c, plane].astype(F32)

            part[c, plane] = total_part[...].astype(BF16)

            @pl.when(plane > z)
            def _():
                part_up(c, plane).start()

            @pl.when(plane < z)
            def _():
                part_down(c, plane).start()

            return carry

        lax.fori_loop(1, PLANES, send, 0)
        home[c] = hidden[:, cols(c)].astype(F32) + combined(c, z)

    def finish(c):
        @pl.when(z > 0)
        def _():
            part_up(c, z).wait_recv()
            home[c] += from_below[c, z].astype(F32)

        @pl.when(z < PLANES - 1)
        def _():
            part_down(c, z).wait_recv()
            home[c] += from_above[c, z].astype(F32)

        layer_out[c] = home[c].astype(BF16)
        hand_copy(c).start()

    def dispatch_left(c, carry):
        def sent_plane(plane, carry):
            go_all(c, plane).wait_send()
            pass_on(c, plane, lambda copy: copy.wait_send())
            return carry

        lax.fori_loop(0, PLANES, sent_plane, 0)
        return carry

    def back_left(c):
        down_copy(c).wait_send()

        def sent_plane(plane, carry):
            back_all(c, plane).wait_send()
            return carry

        lax.fori_loop(0, PLANES, sent_plane, 0)
        for i in range(1, PLANES):
            part_up(c, lax.rem(z + i, PLANES)).wait_send()

    def way_back(c, carry):
        @pl.when(c + AHEAD < BACK_PIECES)
        def _():
            down(c + AHEAD)

        combine(c)

        @pl.when(c > 0)
        def _():
            finish(c - 1)
            back_left(c - 1)

        return carry

    for c in range(AHEAD):
        down(c)
    lax.fori_loop(0, PIECES, dispatch_left, 0)
    for i in range(1, PLANES):
        meta_copy(lax.rem(z + i, PLANES), z).wait_send()
    lax.fori_loop(0, BACK_PIECES, way_back, 0)
    finish(BACK_PIECES - 1)
    back_left(BACK_PIECES - 1)

    for c in range(BACK_PIECES):
        hand_copy(c).wait()


def local(hidden_rows, norm_gain, routes, gates, w_gate_up, w_down):
    hidden = hidden_rows[0]
    tokens, width = hidden.shape
    picks = routes.shape[2]
    cap = tokens * picks // EXPERTS
    inner = w_down.shape[2]
    span = width // PIECES
    back_span = width // BACK_PIECES
    slots = EXPERTS * cap
    hbm = pl.BlockSpec(memory_space=pltpu.HBM)
    dma = pltpu.SemaphoreType.DMA
    blocks = pltpu.VMEM((PIECES, PLANES, EXPERTS, cap, span), BF16)
    per_plane = pltpu.VMEM((PIECES, PLANES, tokens, span), BF16)
    back_blocks = pltpu.VMEM((BACK_PIECES, PLANES, EXPERTS, cap, back_span), BF16)
    back_per_plane = pltpu.VMEM((BACK_PIECES, PLANES, tokens, back_span), BF16)
    handoff = pl.pallas_call(
        layer_kernel,
        out_shape=jax.ShapeDtypeStruct((tokens, width), BF16),
        in_specs=[hbm] * 6,
        out_specs=hbm,
        scratch_shapes=[
            pltpu.VMEM((tokens, width), BF16),
            pltpu.VMEM((1, width), F32),
            pltpu.VMEM((picks, tokens), jnp.int32),
            pltpu.VMEM((picks, tokens), F32),
            per_plane,
            pltpu.VMEM((PLANES, 8, 2 * tokens), F32),
            blocks,
            blocks,
            pltpu.VMEM((2, width, 2 * inner), BF16),
            pltpu.VMEM((BACK_PIECES, 2 * inner, back_span), BF16),
            pltpu.VMEM((2, PLANES * slots, 2 * inner), F32),
            pltpu.VMEM((PLANES * slots, 2 * inner), BF16),
            back_blocks,
            back_blocks,
            back_per_plane,
            back_per_plane,
            back_per_plane,
            pltpu.VMEM((tokens, back_span), F32),
            pltpu.VMEM((BACK_PIECES, tokens, back_span), F32),
            pltpu.VMEM((BACK_PIECES, tokens, back_span), BF16),
            pltpu.VMEM((PLANES, 2 * tokens, slots), BF16),
            dma((5 + BACK_PIECES,)),
            dma((PIECES,)),
            dma((PIECES,)),
            dma((BACK_PIECES,)),
            dma((BACK_PIECES,)),
            dma((PIECES * PLANES,)),
            dma((PIECES * PLANES,)),
            dma((PIECES * PLANES,)),
            dma((PLANES,)),
            dma((PLANES,)),
            dma((PIECES * PLANES,)),
            dma((PIECES * PLANES,)),
            dma((BACK_PIECES * PLANES,)),
            dma((BACK_PIECES * PLANES,)),
            dma((BACK_PIECES * PLANES,)),
            dma((BACK_PIECES * PLANES,)),
            dma((BACK_PIECES * PLANES,)),
            dma((BACK_PIECES,)),
            dma((BACK_PIECES,)),
        ],
        compiler_params=pltpu.CompilerParams(
            collective_id=0, has_side_effects=True, vmem_limit_bytes=62 * 1024 * 1024
        ),
        cost_estimate=pl.CostEstimate(
            flops=6 * EXPERTS * SHARDS * cap * width * inner,
            bytes_accessed=2 * (tokens * width * 2 + 3 * width * inner),
            transcendentals=EXPERTS * SHARDS * cap * inner,
        ),
    )(hidden, norm_gain, routes[0].T, gates[0].T, w_gate_up[0, 0], w_down[0, 0])
    return handoff[None]


def solution(mesh):
    in_specs = (
        P("section", "expert", None),
        P("section", None),
        P("section", "expert", None),
        P("section", "expert", None),
        P("section", "expert", None, None),
        P("section", "expert", None, None),
    )
    out_specs = P("section", "expert", None)
    return jax.shard_map(local, mesh=mesh, in_specs=in_specs, out_specs=out_specs, check_vma=False)
```
